128 devices in a mesh: seq: 16 (over x, z_lo, core), head: 8 (over y, z_hi).
Axes of the slice: x: 4, y: 4, z: 4 (z_hi: 2, z_lo: 2; z = z_hi * 2 + z_lo), core: 2. Of those that a mesh axis runs over, the one named last changes fastest.
Arguments:
- q_nope: bfloat16 [4096, 16384], P('seq', 'head'), may hold values from -6 to 6
- q_rope: bfloat16 [4096, 8192], P('seq', 'head'), may hold values from -120 to 120
- latent: bfloat16 [4096, 512], P(('seq', 'head')), may hold values from -6 to 6
- k_rope: bfloat16 [4096, 64], P(('seq', 'head')), may hold values from -4 to 4
- positions: int32 [4096], P('seq'), may hold values from 0 to 4095, as said below
- w_uk: bfloat16 [512, 16384], P(None, 'head'), may hold values from -0.25 to 0.25
- w_uv: bfloat16 [512, 16384], P(None, 'head'), may hold values from -0.25 to 0.25
Outputs:
- attended: bfloat16 [4096, 16384], P('seq', 'head')
The draws below stay inside these ranges and needn't reach their ends.
Inputs may be any that keep to these rules, and one draw needn't show every extreme that they name: positions is a permutation of 0 to 4095 made of 32 aligned runs of 128 rows, each run holding 128 consecutive rising positions; which block sits where is drawn.
All inputs are finite; a program needn't handle non-finite values.
Results may differ from the reference program's by a relative error of at most 0.0073.
Values may be sent and summed in bfloat16 or wider, within the bound.
A program may use at most 64 MiB of HBM per device.

```python
import jax
import jax.numpy as jnp
from jax import lax

H = 128
NOPE = 128
ROPE = 64
VDIM = 128
LATENT = 512
TOKENS = 4096
BLK = 128
BLOCKS = 32


def draw_k_rope(key, part):
    key = jax.random.fold_in(key, 11)
    result = jnp.clip(jax.random.normal(key, (TOKENS, ROPE), jnp.float32), -4.0, 4.0)
    return result.astype(jnp.bfloat16)


def draw_q_rope(key, part):
    key = jax.random.fold_in(key, 13)
    result = jnp.clip(jax.random.normal(key, (TOKENS, H * ROPE), jnp.float32), -4.0, 4.0)
    return result.astype(jnp.bfloat16)


def draw_positions(key, part):
    key = jax.random.fold_in(key, 17)
    order = jax.random.permutation(key, jnp.arange(BLOCKS, dtype=jnp.int32))
    rows = jnp.arange(TOKENS, dtype=jnp.int32)
    return (order[rows // BLK] * BLK + rows % BLK).astype(jnp.int32)


def block_scale(own_key, extent, cuts, least, top_value):
    def one(dim, parts):
        steps = jax.random.uniform(jax.random.fold_in(jax.random.fold_in(own_key, 6), dim), (parts,), jnp.float32, least / len(cuts), top_value / len(cuts))
        return jnp.repeat(jnp.exp(steps), extent[dim] // parts).reshape((-1,) + (1,) * (len(extent) - dim - 1))

    loudness = one(*cuts[0])
    for cut in cuts[1:]:
        loudness = loudness * one(*cut)
    return loudness


def noise(rng, dims, spread, bound, pieces=(), kind=jnp.bfloat16):
    entries = jax.random.normal(rng, dims, jnp.float32) * spread
    if len(pieces) > 0:
        entries = block_scale(rng, dims, pieces, -0.22, 0.18) * entries
    return jnp.clip(entries, min=-bound, max=bound).astype(kind)


def setup_inputs(seed: int = 0) -> dict:
    streams_of = jax.random.split(jax.random.key(seed), 8)
    return {
        "q_nope": noise(streams_of[0], (TOKENS, H * NOPE), 1.0, 6.0, ((0, 16), (1, 8))),
        "q_rope": draw_q_rope(jax.random.fold_in(streams_of[7], 71), 0),
        "latent": noise(streams_of[2], (TOKENS, LATENT), 1.0, 6.0, ((0, 128),)),
        "k_rope": draw_k_rope(jax.random.fold_in(streams_of[7], 71), 0),
        "positions": draw_positions(jax.random.fold_in(streams_of[7], 71), 0),
        "w_uk": noise(streams_of[5], (LATENT, H * NOPE), LATENT ** -0.5, 0.25, ((1, 8),)),
        "w_uv": noise(streams_of[6], (LATENT, H * VDIM), LATENT ** -0.5, 0.25, ((1, 8),)),
    }


def reference(q_nope, q_rope, latent, k_rope, positions, w_uk, w_uv):
    scale = (NOPE + ROPE) ** -0.5
    allowed = positions[None, :] <= positions[:, None]

    def one_head(head):
        start = (head * NOPE).astype(jnp.int32)
        vstart = (head * VDIM).astype(jnp.int32)
        rstart = (head * ROPE).astype(jnp.int32)
        w_key = lax.dynamic_slice_in_dim(w_uk, start, NOPE, 1)
        w_val = lax.dynamic_slice_in_dim(w_uv, vstart, VDIM, 1)
        keys = jnp.dot(latent, w_key, preferred_element_type=jnp.float32).astype(jnp.bfloat16)
        values = jnp.dot(latent, w_val, preferred_element_type=jnp.float32).astype(jnp.bfloat16)
        query_plain = lax.dynamic_slice_in_dim(q_nope, start, NOPE, 1)
        query_rot = lax.dynamic_slice_in_dim(q_rope, rstart, ROPE, 1)
        scores = jnp.dot(query_plain, keys.T, preferred_element_type=jnp.float32)
        scores = (scores + jnp.dot(query_rot, k_rope.T, preferred_element_type=jnp.float32)) * scale
        scores = jnp.where(allowed, scores, -1e30)
        top = jnp.max(scores, axis=1, keepdims=True)
        weights = jnp.where(allowed, jnp.exp(scores - top), 0.0)
        numer = jnp.dot(weights.astype(jnp.bfloat16), values, preferred_element_type=jnp.float32)
        total = jnp.sum(weights, axis=1, keepdims=True)
        return (numer / total).astype(jnp.bfloat16)

    result = lax.map(one_head, jnp.arange(H, dtype=jnp.int32))
    return jnp.transpose(result, (1, 0, 2)).reshape(TOKENS, H * VDIM)
```

```python
import functools
import math

import jax
import jax.numpy as jnp
from jax import lax
from jax.experimental import pallas as pl
from jax.experimental.pallas import tpu as pltpu
from jax.sharding import PartitionSpec as P

MESH = pl.DeviceIdType.MESH
F32 = jnp.float32
BF16 = jnp.bfloat16
NT = (((1,), (1,)), ((), ()))
NOPE = 128
ROPE = 64
LATENT = 512
WIDE = 640
ROWS = 256
CHUNK = 512
UNIT = 32
HEADS = 8
COLS = HEADS * NOPE
SCALE2 = (NOPE + ROPE) ** (-0.5) * math.log2(math.e)
MASKED = -1e30
SLACK = 60.0


def at_rows(start, size, step):
    return pl.ds(pl.multiple_of(start, step), size)


def block_lanes(shape, block, later):
    lane = lax.broadcasted_iota(jnp.int32, shape, 1) - ROPE
    if later:
        return jnp.where((lane > block) & (lane < 32), MASKED, 0.0)
    return jnp.where(lane == block, 1.0, 0.0)


def query_mask(pos_ref):
    top = block_lanes((128, 128), pos_ref[0] // 128, True)
    low = block_lanes((128, 128), pos_ref[128] // 128, True)
    return jnp.concatenate([top, low], 0).astype(BF16)


def gather_attend(
    pos_ref, lat_ref, rot_ref, qn_hbm, qr_hbm, wk_hbm, wv_hbm,
    out_hbm, all_hbm, peak_ref,
    unit, lat, wk, wv, wvt, qn, qr, qmask, qrot, tri, acc, total, shift, done, peak,
    loc_sem, q_send, q_recv, h_send, h_recv, f_send, f_recv, x_send, x_recv, z_send, z_recv,
    d_send, d_recv, o_loc, o_send, o_recv, all_sem,
):
    seq = lax.axis_index("seq")
    head = lax.axis_index("head")
    x, zl, core = seq // 4, (seq // 2) % 2, seq % 2
    y, zh = head // 2, head % 2
    z = zh * 2 + zl
    other = 1 - core

    def seq_at(px, pzl, pc):
        return px * 4 + pzl * 2 + pc

    def chip_x(d):
        return (seq_at((x + d) % 4, zl, core), head)

    def chip_z(d):
        pz = (z + d) % 4
        return (seq_at(x, pz % 2, core), y * 2 + pz // 2)

    def chip_h(d):
        return (seq, (head + d) % 8)

    sibling = (seq_at(x, zl, other), head)
    partners = [chip_h(d) for d in range(1, 8)] + [chip_x(1), chip_x(3), chip_x(2), chip_z(1), chip_z(3), sibling]

    barrier = pltpu.get_barrier_semaphore()
    for p in partners:
        pl.semaphore_signal(barrier, inc=1, device_id=p, device_id_type=MESH)

    mine = at_rows(core * ROWS, ROWS, ROWS)
    mine_cols = at_rows(core * COLS, COLS, COLS)
    their_cols = at_rows(other * COLS, COLS, COLS)
    half_cols = COLS // 2
    local = [
        pltpu.make_async_copy(wv_hbm.at[:, mine_cols], wv, loc_sem.at[0]),
        pltpu.make_async_copy(wk_hbm.at[:, mine_cols], wk, loc_sem.at[1]),
        pltpu.make_async_copy(qn_hbm.at[:, mine_cols], qn.at[mine], loc_sem.at[2]),
        pltpu.make_async_copy(
            qr_hbm.at[:, at_rows(core * half_cols, half_cols, half_cols)], qr.at[mine], loc_sem.at[3]
        ),
    ]
    for c in local:
        c.start()

    unit[:, :LATENT] = lat_ref[...]
    block = jnp.where(head < 4, pos_ref[0] // 128, pos_ref[128] // 128)
    lane = lax.broadcasted_iota(jnp.int32, (UNIT, 128), 1)
    rot = jnp.concatenate([rot_ref[...].astype(F32), jnp.zeros((UNIT, ROPE), F32)], 1)
    unit[:, LATENT:] = jnp.where(lane < ROPE, rot, block_lanes((UNIT, 128), block, False)).astype(BF16)
    qmask[mine] = query_mask(pos_ref)
    own_unit = at_rows(seq * ROWS + head * UNIT, UNIT, UNIT)
    lat[own_unit, :] = unit[...]

    pl.semaphore_wait(barrier, len(partners))

    def remote(src, dst, send, recv, to):
        return pltpu.make_async_remote_copy(
            src_ref=src, dst_ref=dst, send_sem=send, recv_sem=recv, device_id=to, device_id_type=MESH
        )

    def unit_rows(d):
        return lat.at[at_rows(seq * ROWS + ((head + 8 - d) % 8) * UNIT, UNIT, UNIT)]

    def spread(d):
        return remote(unit, lat.at[own_unit], h_send.at[d], h_recv.at[d], chip_h(d))

    def forward_unit(d):
        src = unit_rows(d)
        return remote(src, src, f_send.at[d], f_recv.at[d], sibling)

    def forward_in(d):
        dst = lat.at[at_rows(seq_at(x, zl, other) * ROWS + ((head + 8 - d) % 8) * UNIT, UNIT, UNIT)]
        return remote(dst, dst, f_send.at[d], f_recv.at[d], sibling)

    for d in (4, 2, 6, 1, 7, 3, 5):
        spread(d).start()
    swap = [
        remote(qn_hbm.at[:, their_cols], qn.at[mine], q_send.at[0], q_recv.at[0], sibling),
        remote(
            qr_hbm.at[:, at_rows(other * half_cols, half_cols, half_cols)], qr.at[mine],
            q_send.at[1], q_recv.at[1], sibling,
        ),
        remote(qmask.at[mine], qmask.at[mine], q_send.at[2], q_recv.at[2], sibling),
    ]
    for c in swap:
        c.start()
    theirs = at_rows(other * ROWS, ROWS, ROWS)
    swap_in = [
        remote(qn.at[theirs], qn.at[theirs], q_send.at[0], q_recv.at[0], sibling),
        remote(qr.at[theirs], qr.at[theirs], q_send.at[1], q_recv.at[1], sibling),
        remote(qmask.at[theirs], qmask.at[theirs], q_send.at[2], q_recv.at[2], sibling),
    ]
    forward_unit(0).start()

    key = lax.broadcasted_iota(jnp.int32, (128, 128), 0)
    query = lax.broadcasted_iota(jnp.int32, (128, 128), 1)
    tri[...] = jnp.where(key > query, MASKED, 0.0)
    acc[...] = jnp.zeros_like(acc)
    total[...] = jnp.zeros_like(total)
    local[0].wait()
    for i in range(HEADS):
        wvt[i * 128 : (i + 1) * 128, :] = wv[:, i * 128 : (i + 1) * 128].T
    for c in local[1:]:
        c.wait()
    for c in swap_in:
        c.wait_recv()
    qlane = lax.broadcasted_iota(jnp.int32, (CHUNK, 128), 1)
    mask_rows = qmask[...].astype(F32)
    for pair in range(HEADS // 2):
        both = qr[:, pair * 128 : (pair + 1) * 128].astype(F32)
        qrot[2 * pair] = jnp.where(qlane < ROPE, both, mask_rows).astype(BF16)
        qrot[2 * pair + 1] = jnp.where(qlane < ROPE, pltpu.roll(both, ROPE, 1), mask_rows).astype(BF16)

    for d in (2, 6, 1, 7, 4, 3, 5):
        spread(d).wait_recv()
        forward_unit(d).start()

    def block_ref(px, pzl, pc, start=0, size=ROWS):
        return lat.at[at_rows(seq_at(px, pzl, pc) * ROWS + start, size, 128)]

    own_block = block_ref(x, zl, core)

    def send_x(i):
        return remote(own_block, own_block, x_send.at[i], x_recv.at[i], chip_x((1, 3, 2)[i]))

    def recv_x(i):
        ref = block_ref((x + (3, 1, 2)[i]) % 4, zl, core)
        return remote(ref, ref, x_send.at[i], x_recv.at[i], sibling)

    z_dx = (0, 1, 3, 2)

    def send_z(j, half):
        ref = block_ref((x + z_dx[j]) % 4, zl, core, half * 128, 128)
        return remote(ref, ref, z_send.at[j, half], z_recv.at[j, half], chip_z((1, 3)[half]))

    def recv_z(j, half):
        ref = block_ref((x + z_dx[j]) % 4, 1 - zl, core, half * 128, 128)
        return remote(ref, ref, z_send.at[j, half], z_recv.at[j, half], sibling)

    order = ((0, 0), (0, 1), (1, 0), (3, 0), (2, 0), (1, 1), (3, 1), (2, 1))

    def pass_on(i):
        dx, dz = order[i]
        ref = block_ref((x + dx) % 4, (zl + dz) % 2, core)
        return remote(ref, ref, d_send.at[i], d_recv.at[i], sibling)

    def pass_in(i):
        dx, dz = order[i]
        ref = block_ref((x + dx) % 4, (zl + dz) % 2, other)
        return remote(ref, ref, d_send.at[i], d_recv.at[i], sibling)

    send_z(0, 0).start()
    send_z(0, 1).start()
    send_x(0).start()
    send_x(1).start()
    for d in range(8):
        forward_in(d).wait_recv()

    def work(index, first):
        rows = at_rows(index * CHUNK, CHUNK, CHUNK)
        made = {}

        def scores(h):
            pair, side = h // 2, h % 2
            if pair not in made:
                cols = slice(pair * 256, (pair + 1) * 256)
                keys = jnp.dot(lat[rows, :LATENT], wk[:, cols], preferred_element_type=F32).astype(BF16)
                vals = lax.dot_general(
                    wvt[cols, :], lat[rows, :LATENT], NT, preferred_element_type=F32
                ).astype(BF16)
                made[pair] = (keys, vals)
            keys = made[pair][0][:, side * 128 : (side + 1) * 128]
            left = jnp.concatenate([keys, lat[rows, LATENT:]], 1)
            right = jnp.concatenate([qn[:, h * 128 : (h + 1) * 128], qrot[h]], 1)
            s = lax.dot_general(left, right, NT, preferred_element_type=F32)
            if first:
                t = tri[...]
                parts = []
                for b in range(4):
                    row = s[b * 128 : (b + 1) * 128]
                    pieces = [row[:, c * 128 : (c + 1) * 128] for c in range(4)]
                    pieces[b] = pieces[b] + t
                    parts.append(jnp.concatenate(pieces, 1))
                s = jnp.concatenate(parts, 0)
            return s

        def finish(h, s):
            s3 = s.reshape(CHUNK // 8, 8, CHUNK)
            if first:
                m = jnp.max(jnp.max(s3, 0), 0, keepdims=True) * SCALE2 + SLACK
                m = jnp.broadcast_to(m, (8, CHUNK))
                shift[h] = m
            else:
                m = shift[h]
            w = jnp.exp2(s3 * SCALE2 - m[None])
            total[h] = total[h] + jnp.sum(w, 0)
            vals = made[h // 2][1][(h % 2) * 128 : (h % 2 + 1) * 128]
            acc[h] = acc[h] + jnp.dot(vals, w.reshape(CHUNK, CHUNK).astype(BF16), preferred_element_type=F32)

        held = scores(0)
        for h in range(HEADS):
            nxt = scores(h + 1) if h + 1 < HEADS else None
            finish(h, held)
            held = nxt

    def keep(index, step):
        rows = at_rows(index * CHUNK, CHUNK, CHUNK)
        return pltpu.make_async_copy(lat.at[rows], all_hbm.at[rows], all_sem.at[step])

    keep(seq // 2, 0).start()
    work(seq // 2, True)

    def step_body(step, carry):
        @pl.when(step == 1)
        def _():
            recv_z(0, 0).wait_recv()
            recv_z(0, 1).wait_recv()
            pass_on(1).start()
            send_x(2).start()
            pass_in(1).wait_recv()

        @pl.when(step == 2)
        def _():
            recv_x(1).wait_recv()
            pass_on(2).start()
            send_z(1, 0).start()
            send_z(1, 1).start()
            recv_x(0).wait_recv()
            pass_on(3).start()
            send_z(2, 0).start()
            send_z(2, 1).start()
            pass_in(2).wait_recv()

        @pl.when(step == 3)
        def _():
            pass_in(3).wait_recv()

        @pl.when(step == 4)
        def _():
            recv_x(2).wait_recv()
            pass_on(4).start()
            send_z(3, 0).start()
            send_z(3, 1).start()
            recv_z(1, 0).wait_recv()
            recv_z(1, 1).wait_recv()
            pass_on(5).start()
            pass_in(4).wait_recv()

        @pl.when(step == 5)
        def _():
            recv_z(2, 0).wait_recv()
            recv_z(2, 1).wait_recv()
            pass_on(6).start()
            pass_in(5).wait_recv()

        @pl.when(step == 6)
        def _():
            recv_z(3, 0).wait_recv()
            recv_z(3, 1).wait_recv()
            pass_on(7).start()
            pass_in(6).wait_recv()

        @pl.when(step == 7)
        def _():
            pass_in(7).wait_recv()

        far = jnp.where(step >= 5, step - 3, step)
        dx = jnp.where(far == 2, 1, jnp.where(far == 3, 3, jnp.where(far == 4, 2, 0)))
        dz = jnp.where(step >= 5, 1, jnp.where(step == 1, 1, 0))
        index = ((x + dx) % 4) * 2 + (zl + dz) % 2
        keep(index, step).start()
        work(index, False)
        return carry

    lax.fori_loop(1, 8, step_body, 0)

    def give(h):
        cols = at_rows(core * COLS + h * 128, 128, 128)
        here = slice(h * 128, (h + 1) * 128)
        return (
            pltpu.make_async_copy(done.at[mine, here], out_hbm.at[:, cols], o_loc.at[h]),
            remote(done.at[theirs, here], out_hbm.at[:, cols], o_send.at[h], o_recv.at[h], sibling),
        )

    most = None
    for h in range(HEADS):
        row = jnp.sum(total[h], 0, keepdims=True)
        most = row if most is None else jnp.maximum(most, row)
        done[:, h * 128 : (h + 1) * 128] = (acc[h] / row).T.astype(BF16)
        for c in give(h):
            c.start()
    peak[0] = jnp.broadcast_to(most[:, :ROWS], (8, ROWS))
    peak[1] = jnp.broadcast_to(most[:, ROWS:], (8, ROWS))
    tell = remote(peak.at[other], peak_ref.at[core], o_send.at[HEADS], o_recv.at[HEADS], sibling)
    tell.start()
    peak_ref[core] = peak[core]

    for c in swap:
        c.wait_send()
    for d in range(1, 8):
        spread(d).wait_send()
    for d in range(8):
        forward_unit(d).wait_send()
    for i in range(3):
        send_x(i).wait_send()
    for j in range(4):
        for half in range(2):
            send_z(j, half).wait_send()
    for i in range(1, 8):
        pass_on(i).wait_send()
    for i in range(8):
        keep(0, i).wait()
    for h in range(HEADS):
        here, there = give(h)
        here.wait()
        there.wait_send()
        cols = at_rows(other * COLS + h * 128, 128, 128)
        into = out_hbm.at[:, cols]
        remote(into, into, o_send.at[h], o_recv.at[h], sibling).wait_recv()
    tell.wait_send()
    into = peak_ref.at[other]
    remote(into, into, o_send.at[HEADS], o_recv.at[HEADS], sibling).wait_recv()


def settle(
    peak_ref, pos_ref, fast_hbm, all_hbm, qn_hbm, qr_hbm, wk_hbm, wv_hbm, out_hbm,
    lat, wk, wv, qn, qr, acc, total, top, result, sem,
):
    whole = pltpu.make_async_copy(fast_hbm, out_hbm, sem)
    whole.start()
    whole.wait()
    bad = jnp.logical_not(jnp.max(peak_ref[...]) <= 1.0)

    @pl.when(bad)
    def _():
        seq = lax.axis_index("seq")
        core = seq % 2

        def fetch(src, dst):
            c = pltpu.make_async_copy(src, dst, sem)
            c.start()
            c.wait()

        fetch(all_hbm, lat)
        qmask = query_mask(pos_ref).astype(F32)
        qlane = lax.broadcasted_iota(jnp.int32, (ROWS, 128), 1)

        def one_pair(pair, carry):
            pair_cols = at_rows(pair * 256, 256, 256)
            fetch(wk_hbm.at[:, pair_cols], wk)
            fetch(wv_hbm.at[:, pair_cols], wv)
            fetch(qn_hbm.at[:, pair_cols], qn)
            fetch(qr_hbm.at[:, at_rows(pair * 128, 128, 128)], qr)
            for side in range(2):
                cols = slice(side * 128, (side + 1) * 128)
                both = qr[...].astype(F32)
                if side:
                    both = pltpu.roll(both, ROPE, 1)
                rot = jnp.where(qlane < ROPE, both, qmask).astype(BF16)
                right = jnp.concatenate([qn[:, cols], rot], 1)
                acc[...] = jnp.zeros_like(acc)
                total[...] = jnp.zeros_like(total)
                top[...] = jnp.full_like(top, MASKED)

                def one_block(i, c):
                    index = (seq + i) % 16
                    rows = at_rows(index * ROWS, ROWS, ROWS)
                    here = lat[rows, :LATENT]
                    keys = jnp.dot(here, wk[:, cols], preferred_element_type=F32).astype(BF16)
                    vals = jnp.dot(here, wv[:, cols], preferred_element_type=F32).astype(BF16)
                    left = jnp.concatenate([keys, lat[rows, LATENT:]], 1)
                    s = lax.dot_general(right, left, NT, preferred_element_type=F32)
                    q = lax.broadcasted_iota(jnp.int32, (ROWS, ROWS), 0)
                    k = lax.broadcasted_iota(jnp.int32, (ROWS, ROWS), 1)
                    hidden = (i == 0) & (q // 128 == k // 128) & (k > q)
                    s = jnp.where(hidden, MASKED, s) * SCALE2
                    new = jnp.maximum(top[...], jnp.max(s, 1, keepdims=True))
                    w = jnp.exp2(s - new[:, :1])
                    factor = jnp.exp2(top[...] - new)
                    total[...] = total[...] * factor + jnp.sum(w, 1, keepdims=True)
                    acc[...] = acc[...] * factor + jnp.dot(w.astype(BF16), vals, preferred_element_type=F32)
                    top[...] = new
                    return c

                lax.fori_loop(0, 16, one_block, 0)
                result[:, cols] = (acc[...] / total[...]).astype(BF16)
            fetch(result, out_hbm.at[:, pair_cols])
            return carry

        lax.fori_loop(0, 8, one_pair, 0)


def per_device(q_nope, q_rope, latent, k_rope, positions, w_uk, w_uv):
    any_spec = pl.BlockSpec(memory_space=pl.ANY)
    vmem = pl.BlockSpec(memory_space=pltpu.VMEM)
    smem = pl.BlockSpec(memory_space=pltpu.SMEM)
    tokens = ROWS * 16
    dma = pltpu.SemaphoreType.DMA
    fast, rows, peak = pl.pallas_call(
        gather_attend,
        out_shape=(
            jax.ShapeDtypeStruct((ROWS, 2 * COLS), BF16),
            jax.ShapeDtypeStruct((tokens, WIDE), BF16),
            jax.ShapeDtypeStruct((2, 8, ROWS), F32),
        ),
        in_specs=[smem, vmem, vmem] + [any_spec] * 4,
        out_specs=(any_spec, any_spec, vmem),
        scratch_shapes=[
            pltpu.VMEM((UNIT, WIDE), BF16),
            pltpu.VMEM((tokens, WIDE), BF16),
            pltpu.VMEM((LATENT, COLS), BF16),
            pltpu.VMEM((LATENT, COLS), BF16),
            pltpu.VMEM((COLS, LATENT), BF16),
            pltpu.VMEM((CHUNK, COLS), BF16),
            pltpu.VMEM((CHUNK, COLS // 2), BF16),
            pltpu.VMEM((CHUNK, 128), BF16),
            pltpu.VMEM((HEADS, CHUNK, 128), BF16),
            pltpu.VMEM((128, 128), F32),
            pltpu.VMEM((HEADS, 128, CHUNK), F32),
            pltpu.VMEM((HEADS, 8, CHUNK), F32),
            pltpu.VMEM((HEADS, 8, CHUNK), F32),
            pltpu.VMEM((CHUNK, COLS), BF16),
            pltpu.VMEM((2, 8, ROWS), F32),
            dma((4,)),
            dma((3,)), dma((3,)),
            dma((8,)), dma((8,)),
            dma((8,)), dma((8,)),
            dma((3,)), dma((3,)),
            dma((4, 2)), dma((4, 2)),
            dma((8,)), dma((8,)),
            dma((HEADS,)),
            dma((HEADS + 1,)), dma((HEADS + 1,)),
            dma((8,)),
        ],
        compiler_params=pltpu.CompilerParams(
            collective_id=0, has_side_effects=True, vmem_limit_bytes=56 * 2**20
        ),
        cost_estimate=pl.CostEstimate(flops=26 * 10**9, bytes_accessed=12 * 2**20, transcendentals=17 * 10**6),
        name="gather_attend",
    )(positions, latent, k_rope, q_nope, q_rope, w_uk, w_uv)
    return pl.pallas_call(
        settle,
        out_shape=jax.ShapeDtypeStruct((ROWS, 2 * COLS), BF16),
        in_specs=[vmem, smem] + [any_spec] * 6,
        out_specs=any_spec,
        scratch_shapes=[
            pltpu.VMEM((tokens, WIDE), BF16),
            pltpu.VMEM((LATENT, 256), BF16),
            pltpu.VMEM((LATENT, 256), BF16),
            pltpu.VMEM((ROWS, 256), BF16),
            pltpu.VMEM((ROWS, 128), BF16),
            pltpu.VMEM((ROWS, 128), F32),
            pltpu.VMEM((ROWS, 128), F32),
            pltpu.VMEM((ROWS, 128), F32),
            pltpu.VMEM((ROWS, 256), BF16),
            pltpu.SemaphoreType.DMA,
        ],
        compiler_params=pltpu.CompilerParams(vmem_limit_bytes=32 * 2**20),
        name="settle",
    )(peak, positions, fast, rows, q_nope, q_rope, w_uk, w_uv)


def solution(mesh):
    in_specs = (
        P("seq", "head"),
        P("seq", "head"),
        P(("seq", "head"), None),
        P(("seq", "head"), None),
        P("seq"),
        P(None, "head"),
        P(None, "head"),
    )
    return jax.shard_map(
        per_device, mesh=mesh, in_specs=in_specs, out_specs=P("seq", "head"), check_vma=False
    )
```

```python
import functools
import math

import jax
import jax.numpy as jnp
from jax import lax
from jax.experimental import pallas as pl
from jax.experimental.pallas import tpu as pltpu
from jax.sharding import PartitionSpec as P

MESH = pl.DeviceIdType.MESH
F32 = jnp.float32
BF16 = jnp.bfloat16
NT = (((1,), (1,)), ((), ()))
NOPE = 128
ROPE = 64
LATENT = 512
WIDE = 640
ROWS = 256
CHUNK = 512
UNIT = 32
HEADS = 8
COLS = HEADS * NOPE
SCALE2 = (NOPE + ROPE) ** (-0.5) * math.log2(math.e)
MASKED = -1e30
SLACK = 60.0


def at_rows(start, size, step):
    return pl.ds(pl.multiple_of(start, step), size)


def block_lanes(shape, block, later):
    lane = lax.broadcasted_iota(jnp.int32, shape, 1) - ROPE
    if later:
        return jnp.where((lane > block) & (lane < 32), MASKED, 0.0)
    return jnp.where(lane == block, 1.0, 0.0)


def query_mask(pos_ref):
    top = block_lanes((128, 128), pos_ref[0] // 128, True)
    low = block_lanes((128, 128), pos_ref[128] // 128, True)
    return jnp.concatenate([top, low], 0).astype(BF16)


def gather_attend(
    pos_ref, lat_ref, rot_ref, qn_hbm, qr_hbm, wk_hbm, wv_hbm,
    out_hbm, all_hbm, peak_ref,
    unit, lat, wk, wv, wvt, qn, qr, qmask, qrot, tri, acc, total, shift, done, peak,
    loc_sem, q_send, q_recv, h_send, h_recv, f_send, f_recv, x_send, x_recv, far_send, far_recv,
    u_send, u_recv, z_send, z_recv, d_send, d_recv, o_loc, o_send, o_recv, all_sem,
):
    seq = lax.axis_index("seq")
    head = lax.axis_index("head")
    x, zl, core = seq // 4, (seq // 2) % 2, seq % 2
    y, zh = head // 2, head % 2
    z = zh * 2 + zl
    other = 1 - core

    def seq_at(px, pzl, pc):
        return px * 4 + pzl * 2 + pc

    def chip_x(d):
        return (seq_at((x + d) % 4, zl, core), head)

    def chip_z(d):
        pz = (z + d) % 4
        return (seq_at(x, pz % 2, core), y * 2 + pz // 2)

    def chip_h(i):
        dy, dzh = i // 2, i % 2
        return (seq, ((y + dy) % 4) * 2 + (zh + dzh) % 2)

    sibling = (seq_at(x, zl, other), head)
    partners = [chip_h(i) for i in range(1, 8)] + [chip_x(1), chip_x(3), chip_z(1), chip_z(3), sibling]

    barrier = pltpu.get_barrier_semaphore()
    for p in partners:
        pl.semaphore_signal(barrier, inc=1, device_id=p, device_id_type=MESH)

    mine = at_rows(core * ROWS, ROWS, ROWS)
    mine_cols = at_rows(core * COLS, COLS, COLS)
    their_cols = at_rows(other * COLS, COLS, COLS)
    half_cols = COLS // 2
    local = [
        pltpu.make_async_copy(wv_hbm.at[:, mine_cols], wv, loc_sem.at[0]),
        pltpu.make_async_copy(wk_hbm.at[:, mine_cols], wk, loc_sem.at[1]),
        pltpu.make_async_copy(qn_hbm.at[:, mine_cols], qn.at[mine], loc_sem.at[2]),
        pltpu.make_async_copy(
            qr_hbm.at[:, at_rows(core * half_cols, half_cols, half_cols)], qr.at[mine], loc_sem.at[3]
        ),
    ]
    for c in local:
        c.start()

    unit[:, :LATENT] = lat_ref[...]
    block = jnp.where(head < 4, pos_ref[0] // 128, pos_ref[128] // 128)
    lane = lax.broadcasted_iota(jnp.int32, (UNIT, 128), 1)
    rot = jnp.concatenate([rot_ref[...].astype(F32), jnp.zeros((UNIT, ROPE), F32)], 1)
    unit[:, LATENT:] = jnp.where(lane < ROPE, rot, block_lanes((UNIT, 128), block, False)).astype(BF16)
    qmask[mine] = query_mask(pos_ref)
    own_unit = at_rows(seq * ROWS + head * UNIT, UNIT, UNIT)
    lat[own_unit, :] = unit[...]

    pl.semaphore_wait(barrier, len(partners))

    def remote(src, dst, send, recv, to):
        return pltpu.make_async_remote_copy(
            src_ref=src, dst_ref=dst, send_sem=send, recv_sem=recv, device_id=to, device_id_type=MESH
        )

    def unit_ref(sq, i, own_zh):
        h = ((y + 4 - i // 2) % 4) * 2 + (own_zh + i) % 2
        return lat.at[at_rows(sq * ROWS + h * UNIT, UNIT, UNIT)]

    def spread(i):
        return remote(unit, lat.at[own_unit], h_send.at[i], h_recv.at[i], chip_h(i))

    def spread_in(i):
        ref = unit_ref(seq, i, zh)
        return remote(ref, ref, h_send.at[i], h_recv.at[i], sibling)

    def forward_unit(i):
        src = unit_ref(seq, i, zh)
        return remote(src, src, f_send.at[i], f_recv.at[i], sibling)

    def forward_in(i):
        dst = unit_ref(seq_at(x, zl, other), i, zh)
        return remote(dst, dst, f_send.at[i], f_recv.at[i], sibling)

    def unit_x(i, way):
        src = unit_ref(seq, i, zh)
        return remote(src, src, x_send.at[way, i], x_recv.at[way, i], chip_x((1, 3)[way]))

    def unit_x_in(i, way):
        dst = unit_ref(seq_at((x + (3, 1)[way]) % 4, zl, core), i, zh)
        return remote(dst, dst, x_send.at[way, i], x_recv.at[way, i], sibling)

    def unit_z(i):
        src = unit_ref(seq, i, zh)
        return remote(src, src, u_send.at[i], u_recv.at[i], chip_z((1, 3)[(i // 2) % 2]))

    def unit_z_in(i):
        from_zh = ((z + (3, 1)[(i // 2) % 2]) % 4) // 2
        dst = unit_ref(seq_at(x, 1 - zl, core), i, from_zh)
        return remote(dst, dst, u_send.at[i], u_recv.at[i], sibling)

    for i in (1, 5, 3, 7, 4, 2, 6):
        spread(i).start()
    unit_x(0, 0).start()
    unit_x(0, 1).start()
    swap = [
        remote(qn_hbm.at[:, their_cols], qn.at[mine], q_send.at[0], q_recv.at[0], sibling),
        remote(
            qr_hbm.at[:, at_rows(other * half_cols, half_cols, half_cols)], qr.at[mine],
            q_send.at[1], q_recv.at[1], sibling,
        ),
        remote(qmask.at[mine], qmask.at[mine], q_send.at[2], q_recv.at[2], sibling),
    ]
    for c in swap:
        c.start()
    theirs = at_rows(other * ROWS, ROWS, ROWS)
    swap_in = [
        remote(qn.at[theirs], qn.at[theirs], q_send.at[0], q_recv.at[0], sibling),
        remote(qr.at[theirs], qr.at[theirs], q_send.at[1], q_recv.at[1], sibling),
        remote(qmask.at[theirs], qmask.at[theirs], q_send.at[2], q_recv.at[2], sibling),
    ]
    forward_unit(0).start()
    unit_z(0).start()

    key = lax.broadcasted_iota(jnp.int32, (128, 128), 0)
    query = lax.broadcasted_iota(jnp.int32, (128, 128), 1)
    tri[...] = jnp.where(key > query, MASKED, 0.0)
    acc[...] = jnp.zeros_like(acc)
    total[...] = jnp.zeros_like(total)
    local[0].wait()
    for i in range(HEADS):
        wvt[i * 128 : (i + 1) * 128, :] = wv[:, i * 128 : (i + 1) * 128].T
    for c in local[1:]:
        c.wait()
    for c in swap_in:
        c.wait_recv()
    qlane = lax.broadcasted_iota(jnp.int32, (CHUNK, 128), 1)
    mask_rows = qmask[...].astype(F32)
    for pair in range(HEADS // 2):
        both = qr[:, pair * 128 : (pair + 1) * 128].astype(F32)
        qrot[2 * pair] = jnp.where(qlane < ROPE, both, mask_rows).astype(BF16)
        qrot[2 * pair + 1] = jnp.where(qlane < ROPE, pltpu.roll(both, ROPE, 1), mask_rows).astype(BF16)

    for i in (2, 6, 4, 1, 3, 7, 5):
        spread_in(i).wait_recv()
        forward_unit(i).start()
        unit_z(i).start()
        unit_x(i, 0).start()
        unit_x(i, 1).start()

    def block_ref(px, pzl, pc, start=0, size=ROWS):
        return lat.at[at_rows(seq_at(px, pzl, pc) * ROWS + start, size, 128)]

    def send_far(half):
        ref = block_ref((x + (3, 1)[half]) % 4, zl, core, half * 128, 128)
        return remote(ref, ref, far_send.at[half], far_recv.at[half], chip_x((1, 3)[half]))

    def recv_far(half):
        ref = block_ref((x + 2) % 4, zl, core, half * 128, 128)
        return remote(ref, ref, far_send.at[half], far_recv.at[half], sibling)

    z_dx = (0, 1, 3, 2)

    def send_z(j, half):
        ref = block_ref((x + z_dx[j]) % 4, zl, core, half * 128, 128)
        return remote(ref, ref, z_send.at[j, half], z_recv.at[j, half], chip_z((1, 3)[half]))

    def recv_z(j, half):
        ref = block_ref((x + z_dx[j]) % 4, 1 - zl, core, half * 128, 128)
        return remote(ref, ref, z_send.at[j, half], z_recv.at[j, half], sibling)

    order = ((0, 0), (0, 1), (1, 0), (3, 0), (2, 0), (1, 1), (3, 1), (2, 1))

    def pass_on(i):
        dx, dz = order[i]
        ref = block_ref((x + dx) % 4, (zl + dz) % 2, core)
        return remote(ref, ref, d_send.at[i], d_recv.at[i], sibling)

    def pass_in(i):
        dx, dz = order[i]
        ref = block_ref((x + dx) % 4, (zl + dz) % 2, other)
        return remote(ref, ref, d_send.at[i], d_recv.at[i], sibling)

    for i in range(8):
        forward_in(i).wait_recv()

    def work(index, first):
        rows = at_rows(index * CHUNK, CHUNK, CHUNK)
        made = {}

        def scores(h):
            pair, side = h // 2, h % 2
            if pair not in made:
                cols = slice(pair * 256, (pair + 1) * 256)
                keys = jnp.dot(lat[rows, :LATENT], wk[:, cols], preferred_element_type=F32).astype(BF16)
                vals = lax.dot_general(
                    wvt[cols, :], lat[rows, :LATENT], NT, preferred_element_type=F32
                ).astype(BF16)
                made[pair] = (keys, vals)
            keys = made[pair][0][:, side * 128 : (side + 1) * 128]
            left = jnp.concatenate([keys, lat[rows, LATENT:]], 1)
            right = jnp.concatenate([qn[:, h * 128 : (h + 1) * 128], qrot[h]], 1)
            s = lax.dot_general(left, right, NT, preferred_element_type=F32)
            if first:
                t = tri[...]
                parts = []
                for b in range(4):
                    row = s[b * 128 : (b + 1) * 128]
                    pieces = [row[:, c * 128 : (c + 1) * 128] for c in range(4)]
                    pieces[b] = pieces[b] + t
                    parts.append(jnp.concatenate(pieces, 1))
                s = jnp.concatenate(parts, 0)
            return s

        def finish(h, s):
            s3 = s.reshape(CHUNK // 8, 8, CHUNK)
            if first:
                m = jnp.max(jnp.max(s3, 0), 0, keepdims=True) * SCALE2 + SLACK
                m = jnp.broadcast_to(m, (8, CHUNK))
                shift[h] = m
            else:
                m = shift[h]
            w = jnp.exp2(s3 * SCALE2 - m[None])
            total[h] = total[h] + jnp.sum(w, 0)
            vals = made[h // 2][1][(h % 2) * 128 : (h % 2 + 1) * 128]
            acc[h] = acc[h] + jnp.dot(vals, w.reshape(CHUNK, CHUNK).astype(BF16), preferred_element_type=F32)

        held = scores(0)
        for h in range(HEADS):
            nxt = scores(h + 1) if h + 1 < HEADS else None
            finish(h, held)
            held = nxt

    def keep(index, step):
        rows = at_rows(index * CHUNK, CHUNK, CHUNK)
        return pltpu.make_async_copy(lat.at[rows], all_hbm.at[rows], all_sem.at[step])

    keep(seq // 2, 0).start()
    work(seq // 2, True)

    def step_body(step, carry):
        @pl.when(step == 1)
        def _():
            for i in range(8):
                unit_z_in(i).wait_recv()
            pass_on(1).start()
            for way in (1, 0):
                for i in range(8):
                    unit_x_in(i, way).wait_recv()
                send_far(way).start()
                pass_on((3, 2)[way]).start()
                send_z((2, 1)[way], 0).start()
                send_z((2, 1)[way], 1).start()
            pass_in(1).wait_recv()

        @pl.when(step == 2)
        def _():
            pass_in(2).wait_recv()

        @pl.when(step == 3)
        def _():
            recv_far(0).wait_recv()
            recv_far(1).wait_recv()
            pass_on(4).start()
            send_z(3, 0).start()
            send_z(3, 1).start()
            pass_in(3).wait_recv()

        @pl.when(step == 4)
        def _():
            recv_z(1, 0).wait_recv()
            recv_z(1, 1).wait_recv()
            pass_on(5).start()
            pass_in(4).wait_recv()

        @pl.when(step == 5)
        def _():
            recv_z(2, 0).wait_recv()
            recv_z(2, 1).wait_recv()
            pass_on(6).start()
            pass_in(5).wait_recv()

        @pl.when(step == 6)
        def _():
            recv_z(3, 0).wait_recv()
            recv_z(3, 1).wait_recv()
            pass_on(7).start()
            pass_in(6).wait_recv()

        @pl.when(step == 7)
        def _():
            pass_in(7).wait_recv()

        far = jnp.where(step >= 5, step - 3, step)
        dx = jnp.where(far == 2, 1, jnp.where(far == 3, 3, jnp.where(far == 4, 2, 0)))
        dz = jnp.where(step >= 5, 1, jnp.where(step == 1, 1, 0))
        index = ((x + dx) % 4) * 2 + (zl + dz) % 2
        keep(index, step).start()
        work(index, False)
        return carry

    lax.fori_loop(1, 8, step_body, 0)

    def give(h):
        cols = at_rows(core * COLS + h * 128, 128, 128)
        here = slice(h * 128, (h + 1) * 128)
        return (
            pltpu.make_async_copy(done.at[mine, here], out_hbm.at[:, cols], o_loc.at[h]),
            remote(done.at[theirs, here], out_hbm.at[:, cols], o_send.at[h], o_recv.at[h], sibling),
        )

    most = None
    for h in range(HEADS):
        row = jnp.sum(total[h], 0, keepdims=True)
        most = row if most is None else jnp.maximum(most, row)
        done[:, h * 128 : (h + 1) * 128] = (acc[h] / row).T.astype(BF16)
        for c in give(h):
            c.start()
    peak[0] = jnp.broadcast_to(most[:, :ROWS], (8, ROWS))
    peak[1] = jnp.broadcast_to(most[:, ROWS:], (8, ROWS))
    tell = remote(peak.at[other], peak_ref.at[core], o_send.at[HEADS], o_recv.at[HEADS], sibling)
    tell.start()
    peak_ref[core] = peak[core]

    for c in swap:
        c.wait_send()
    for i in range(8):
        if i:
            spread(i).wait_send()
        forward_unit(i).wait_send()
        unit_z(i).wait_send()
        unit_x(i, 0).wait_send()
        unit_x(i, 1).wait_send()
    for half in range(2):
        send_far(half).wait_send()
        for j in range(1, 4):
            send_z(j, half).wait_send()
    for i in range(1, 8):
        pass_on(i).wait_send()
    for i in range(8):
        keep(0, i).wait()
    for h in range(HEADS):
        here, there = give(h)
        here.wait()
        there.wait_send()
        cols = at_rows(other * COLS + h * 128, 128, 128)
        into = out_hbm.at[:, cols]
        remote(into, into, o_send.at[h], o_recv.at[h], sibling).wait_recv()
    tell.wait_send()
    into = peak_ref.at[other]
    remote(into, into, o_send.at[HEADS], o_recv.at[HEADS], sibling).wait_recv()


def settle(
    peak_hbm, pos_ref, fast_hbm, all_hbm, qn_hbm, qr_hbm, wk_hbm, wv_hbm, out_hbm,
    peak, lat, wk, wv, qn, qr, acc, total, top, result, sem, peak_sem,
):
    whole = pltpu.make_async_copy(fast_hbm, out_hbm, sem)
    whole.start()
    look = pltpu.make_async_copy(peak_hbm, peak, peak_sem)
    look.start()
    look.wait()
    bad = jnp.logical_not(jnp.max(peak[...]) <= 1.0)
    whole.wait()

    @pl.when(bad)
    def _():
        seq = lax.axis_index("seq")
        core = seq % 2

        def fetch(src, dst):
            c = pltpu.make_async_copy(src, dst, sem)
            c.start()
            c.wait()

        fetch(all_hbm, lat)
        qmask = query_mask(pos_ref).astype(F32)
        qlane = lax.broadcasted_iota(jnp.int32, (ROWS, 128), 1)

        def one_pair(pair, carry):
            pair_cols = at_rows(pair * 256, 256, 256)
            fetch(wk_hbm.at[:, pair_cols], wk)
            fetch(wv_hbm.at[:, pair_cols], wv)
            fetch(qn_hbm.at[:, pair_cols], qn)
            fetch(qr_hbm.at[:, at_rows(pair * 128, 128, 128)], qr)
            for side in range(2):
                cols = slice(side * 128, (side + 1) * 128)
                both = qr[...].astype(F32)
                if side:
                    both = pltpu.roll(both, ROPE, 1)
                rot = jnp.where(qlane < ROPE, both, qmask).astype(BF16)
                right = jnp.concatenate([qn[:, cols], rot], 1)
                acc[...] = jnp.zeros_like(acc)
                total[...] = jnp.zeros_like(total)
                top[...] = jnp.full_like(top, MASKED)

                def one_block(i, c):
                    index = (seq + i) % 16
                    rows = at_rows(index * ROWS, ROWS, ROWS)
                    here = lat[rows, :LATENT]
                    keys = jnp.dot(here, wk[:, cols], preferred_element_type=F32).astype(BF16)
                    vals = jnp.dot(here, wv[:, cols], preferred_element_type=F32).astype(BF16)
                    left = jnp.concatenate([keys, lat[rows, LATENT:]], 1)
                    s = lax.dot_general(right, left, NT, preferred_element_type=F32)
                    q = lax.broadcasted_iota(jnp.int32, (ROWS, ROWS), 0)
                    k = lax.broadcasted_iota(jnp.int32, (ROWS, ROWS), 1)
                    hidden = (i == 0) & (q // 128 == k // 128) & (k > q)
                    s = jnp.where(hidden, MASKED, s) * SCALE2
                    new = jnp.maximum(top[...], jnp.max(s, 1, keepdims=True))
                    w = jnp.exp2(s - new[:, :1])
                    factor = jnp.exp2(top[...] - new)
                    total[...] = total[...] * factor + jnp.sum(w, 1, keepdims=True)
                    acc[...] = acc[...] * factor + jnp.dot(w.astype(BF16), vals, preferred_element_type=F32)
                    top[...] = new
                    return c

                lax.fori_loop(0, 16, one_block, 0)
                result[:, cols] = (acc[...] / total[...]).astype(BF16)
            fetch(result, out_hbm.at[:, pair_cols])
            return carry

        lax.fori_loop(0, 8, one_pair, 0)


def per_device(q_nope, q_rope, latent, k_rope, positions, w_uk, w_uv):
    hbm = pl.BlockSpec(memory_space=pltpu.HBM)
    vmem = pl.BlockSpec(memory_space=pltpu.VMEM)
    smem = pl.BlockSpec(memory_space=pltpu.SMEM)
    tokens = ROWS * 16
    dma = pltpu.SemaphoreType.DMA
    fast, rows, peak = pl.pallas_call(
        gather_attend,
        out_shape=(
            jax.ShapeDtypeStruct((ROWS, 2 * COLS), BF16),
            jax.ShapeDtypeStruct((tokens, WIDE), BF16),
            jax.ShapeDtypeStruct((2, 8, ROWS), F32),
        ),
        in_specs=[smem, vmem, vmem] + [hbm] * 4,
        out_specs=(hbm, hbm, vmem),
        scratch_shapes=[
            pltpu.VMEM((UNIT, WIDE), BF16),
            pltpu.VMEM((tokens, WIDE), BF16),
            pltpu.VMEM((LATENT, COLS), BF16),
            pltpu.VMEM((LATENT, COLS), BF16),
            pltpu.VMEM((COLS, LATENT), BF16),
            pltpu.VMEM((CHUNK, COLS), BF16),
            pltpu.VMEM((CHUNK, COLS // 2), BF16),
            pltpu.VMEM((CHUNK, 128), BF16),
            pltpu.VMEM((HEADS, CHUNK, 128), BF16),
            pltpu.VMEM((128, 128), F32),
            pltpu.VMEM((HEADS, 128, CHUNK), F32),
            pltpu.VMEM((HEADS, 8, CHUNK), F32),
            pltpu.VMEM((HEADS, 8, CHUNK), F32),
            pltpu.VMEM((CHUNK, COLS), BF16),
            pltpu.VMEM((2, 8, ROWS), F32),
            dma((4,)),
            dma((3,)), dma((3,)),
            dma((8,)), dma((8,)),
            dma((8,)), dma((8,)),
            dma((2, 8)), dma((2, 8)),
            dma((2,)), dma((2,)),
            dma((8,)), dma((8,)),
            dma((4, 2)), dma((4, 2)),
            dma((8,)), dma((8,)),
            dma((HEADS,)),
            dma((HEADS + 1,)), dma((HEADS + 1,)),
            dma((8,)),
        ],
        compiler_params=pltpu.CompilerParams(
            collective_id=0, has_side_effects=True, vmem_limit_bytes=56 * 2**20
        ),
        cost_estimate=pl.CostEstimate(flops=26 * 10**9, bytes_accessed=12 * 2**20, transcendentals=17 * 10**6),
        name="gather_attend",
    )(positions, latent, k_rope, q_nope, q_rope, w_uk, w_uv)
    return pl.pallas_call(
        settle,
        out_shape=jax.ShapeDtypeStruct((ROWS, 2 * COLS), BF16),
        in_specs=[hbm, smem] + [hbm] * 6,
        out_specs=hbm,
        scratch_shapes=[
            pltpu.VMEM((2, 8, ROWS), F32),
            pltpu.VMEM((tokens, WIDE), BF16),
            pltpu.VMEM((LATENT, 256), BF16),
            pltpu.VMEM((LATENT, 256), BF16),
            pltpu.VMEM((ROWS, 256), BF16),
            pltpu.VMEM((ROWS, 128), BF16),
            pltpu.VMEM((ROWS, 128), F32),
            pltpu.VMEM((ROWS, 128), F32),
            pltpu.VMEM((ROWS, 128), F32),
            pltpu.VMEM((ROWS, 256), BF16),
            pltpu.SemaphoreType.DMA,
            pltpu.SemaphoreType.DMA,
        ],
        compiler_params=pltpu.CompilerParams(vmem_limit_bytes=64 * 2**20 - 2**16),
        name="settle",
    )(peak, positions, fast, rows, q_nope, q_rope, w_uk, w_uv)


def solution(mesh):
    in_specs = (
        P("seq", "head"),
        P("seq", "head"),
        P(("seq", "head"), None),
        P(("seq", "head"), None),
        P("seq"),
        P(None, "head"),
        P(None, "head"),
    )
    return jax.shard_map(
        per_device, mesh=mesh, in_specs=in_specs, out_specs=P("seq", "head"), check_vma=False
    )
```

```python
import functools
import math

import jax
import jax.numpy as jnp
from jax import lax
from jax.experimental import pallas as pl
from jax.experimental.pallas import tpu as pltpu
from jax.sharding import PartitionSpec as P

MESH = pl.DeviceIdType.MESH
F32 = jnp.float32
BF16 = jnp.bfloat16
NT = (((1,), (1,)), ((), ()))
NOPE = 128
ROPE = 64
LATENT = 512
WIDE = 640
ROWS = 256
CHUNK = 512
UNIT = 32
HEADS = 8
AHEAD = 3
COLS = HEADS * NOPE
SCALE2 = (NOPE + ROPE) ** (-0.5) * math.log2(math.e)
MASKED = -1e30
SHIFT = 576.0
LEAST = 2.0**-90


def both_signs(pattern):
    found = [()]
    for p in pattern:
        found = [f + (v,) for f in found for v in ((1, 3) if p == 1 else (p,))]
    return found


SLOTS = (
    [(0, 0, 0), (0, 1, 0), (0, 3, 0), (1, 0, 0), (3, 0, 0), (0, 0, 1), (0, 0, 3), (2, 0, 0)]
    + both_signs((1, 1, 0)) + both_signs((1, 0, 1))
    + both_signs((0, 1, 1)) + both_signs((2, 1, 0)) + both_signs((2, 0, 1))
    + both_signs((1, 2, 0)) + both_signs((0, 2, 1)) + both_signs((1, 0, 2)) + [(2, 2, 0), (2, 0, 2)]
    + both_signs((1, 1, 1))
    + both_signs((2, 1, 1)) + both_signs((1, 2, 1))
    + both_signs((1, 1, 2)) + both_signs((2, 2, 1)) + both_signs((1, 2, 2))
    + [(0, 2, 0), (0, 0, 2), (0, 1, 2), (0, 3, 2), (0, 2, 2), (2, 1, 2), (2, 3, 2), (2, 2, 2)]
)
Y2, Z2 = 56, 57
OWN_FIRST, OWN_LAST = 3, 5
STAGES = (
    list(range(1, 8)) + [Y2, Z2],
    list(range(8, 24)),
    list(range(24, 32)) + [58, 59, 60],
    list(range(32, 44)),
    list(range(44, 56)) + [61, 62, 63],
)


def plan_routes():
    place = {s: i for i, s in enumerate(SLOTS)}
    routes = {i: (SLOTS[i], 0) for i in STAGES[0]}
    first = {0} | set(STAGES[0])
    ready = (first, first, first, first | set(STAGES[1]), first | set(STAGES[1]) | set(range(24, 32)))
    for stages, have in (
        (STAGES[1] + STAGES[2], first),
        (STAGES[3], first | set(STAGES[1])),
        (STAGES[4], first | set(STAGES[1]) | set(range(24, 32))),
    ):
        load = {}
        options, taken = {}, {}
        for i in stages:
            options[i] = []
            for axis in range(3):
                for way in {0: (), 1: (1,), 3: (3,), 2: (1, 3, 2)}[SLOTS[i][axis]]:
                    step = tuple(way if a == axis else 0 for a in range(3))
                    parent = place[tuple((v - w) % 4 for v, w in zip(SLOTS[i], step))]
                    if parent in have:
                        links = [(axis, w) for w in ((1, 3) if way == 2 else (way,))]
                        options[i].append((step, parent, links))
            single = [o for o in options[i] if len(o[2]) == 1]
            options[i] = single or options[i]
        for i in stages * 6:
            for k in taken.get(i, ((), 0, ()))[2]:
                load[k] -= 1
            taken[i] = min(options[i], key=lambda o: (sum(load.get(k, 0) for k in o[2]) / len(o[2]), o[0], o[1]))
            for k in taken[i][2]:
                load[k] = load.get(k, 0) + 1
        for i in stages:
            routes[i] = taken[i][:2]
    return routes


ROUTES = plan_routes()


def at_rows(start, size, step):
    return pl.ds(pl.multiple_of(start, step), size)


def key_lanes(shape, block):
    return jnp.where(lax.broadcasted_iota(jnp.int32, shape, 1) - ROPE == block, 1.0, 0.0)


def query_mask(pos_ref):
    parts = []
    for i in range(2):
        lane = lax.broadcasted_iota(jnp.int32, (128, 128), 1) - ROPE
        value = jnp.where(lane > pos_ref[i * 128] // 128, MASKED, -SHIFT)
        parts.append(jnp.where((lane >= 0) & (lane < 32), value, 0.0))
    return jnp.concatenate(parts, 0).astype(BF16)


def head_of(slot, y, zh):
    _, dy, dz = SLOTS[slot]
    return ((y + dy) % 4) * 2 + (zh + dz // 2) % 2


def gather_attend(
    pos_ref, lat_ref, rot_ref, qn_hbm, qr_hbm, wk_hbm, wv_hbm,
    out_hbm, all_hbm, peak_ref,
    lat, wk, wv, wvt, qn, qr, qmask, qrot, hide, acc, total, done, peak,
    loc_sem, q_send, q_recv, u_send, u_recv, d_send, d_recv, o_loc, o_send, o_recv, all_sem,
):
    seq = lax.axis_index("seq")
    head = lax.axis_index("head")
    x, zl, core = seq // 4, (seq // 2) % 2, seq % 2
    y, zh = head // 2, head % 2
    z = zh * 2 + zl
    other = 1 - core

    def chip(back):
        px, py, pz = (x + 4 - back[0]) % 4, (y + 4 - back[1]) % 4, (z + 4 - back[2]) % 4
        return (px * 4 + (pz % 2) * 2 + core, py * 2 + pz // 2)

    sibling = (seq + 1 - 2 * core, head)
    partners = [chip(SLOTS[i]) for i in STAGES[0]] + [sibling]

    barrier = pltpu.get_barrier_semaphore()
    for p in partners:
        pl.semaphore_signal(barrier, inc=1, device_id=p, device_id_type=MESH)

    mine = at_rows(core * ROWS, ROWS, ROWS)
    theirs = at_rows(other * ROWS, ROWS, ROWS)
    mine_cols = at_rows(core * COLS, COLS, COLS)
    their_cols = at_rows(other * COLS, COLS, COLS)
    half_cols = COLS // 2
    local = [
        pltpu.make_async_copy(wv_hbm.at[:, mine_cols], wv, loc_sem.at[0]),
        pltpu.make_async_copy(wk_hbm.at[:, mine_cols], wk, loc_sem.at[1]),
        pltpu.make_async_copy(qn_hbm.at[:, mine_cols], qn.at[mine], loc_sem.at[2]),
        pltpu.make_async_copy(
            qr_hbm.at[:, at_rows(core * half_cols, half_cols, half_cols)], qr.at[mine], loc_sem.at[3]
        ),
    ]
    for c in local:
        c.start()

    block = jnp.where(head < 4, pos_ref[0] // 128, pos_ref[128] // 128)
    lane = lax.broadcasted_iota(jnp.int32, (UNIT, 128), 1)
    rot = jnp.concatenate([rot_ref[...].astype(F32), jnp.zeros((UNIT, ROPE), F32)], 1)
    lat[0, core, :, :LATENT] = lat_ref[...]
    lat[0, core, :, LATENT:] = jnp.where(lane < ROPE, rot, key_lanes((UNIT, 128), block)).astype(BF16)
    qmask[mine] = query_mask(pos_ref)

    pl.semaphore_wait(barrier, len(partners))

    def remote(src, dst, send, recv, to):
        return pltpu.make_async_remote_copy(
            src_ref=src, dst_ref=dst, send_sem=send, recv_sem=recv, device_id=to, device_id_type=MESH
        )

    def pass_unit(i):
        step, parent = ROUTES[i]
        return remote(lat.at[parent, core], lat.at[i, core], u_send.at[i], u_recv.at[i], chip(step))

    def unit_in(i):
        ref = lat.at[i, core]
        return remote(ref, ref, u_send.at[i], u_recv.at[i], sibling)

    def share(i, size, sem, side):
        ref = lat.at[pl.ds(i, size), side]
        return remote(ref, ref, d_send.at[sem], d_recv.at[sem], sibling)

    def share_chunk(k):
        return share(k * 8, 8, k, core)

    def chunk_in(k):
        return share(k * 8, 8, k, other)

    for i in STAGES[0]:
        pass_unit(i).start()
    swap = [
        remote(qn_hbm.at[:, their_cols], qn.at[mine], q_send.at[0], q_recv.at[0], sibling),
        remote(
            qr_hbm.at[:, at_rows(other * half_cols, half_cols, half_cols)], qr.at[mine],
            q_send.at[1], q_recv.at[1], sibling,
        ),
        remote(qmask.at[mine], qmask.at[mine], q_send.at[2], q_recv.at[2], sibling),
    ]
    for c in swap:
        c.start()
    swap_in = [
        remote(qn.at[theirs], qn.at[theirs], q_send.at[0], q_recv.at[0], sibling),
        remote(qr.at[theirs], qr.at[theirs], q_send.at[1], q_recv.at[1], sibling),
        remote(qmask.at[theirs], qmask.at[theirs], q_send.at[2], q_recv.at[2], sibling),
    ]

    qlane = lax.broadcasted_iota(jnp.int32, (ROWS, 128), 1)

    def prepare(rows):
        mask_rows = qmask[rows].astype(F32)
        for pair in range(HEADS // 2):
            both = qr[rows, pair * 128 : (pair + 1) * 128].astype(F32)
            qrot[2 * pair, rows] = jnp.where(qlane < ROPE, both, mask_rows).astype(BF16)
            qrot[2 * pair + 1, rows] = jnp.where(qlane < ROPE, pltpu.roll(both, ROPE, 1), mask_rows).astype(BF16)

    local[2].wait()
    local[3].wait()
    prepare(mine)
    key = lax.broadcasted_iota(jnp.int32, (UNIT, CHUNK), 0)
    query = lax.broadcasted_iota(jnp.int32, (UNIT, CHUNK), 1)
    for n, slot in enumerate(list(range(OWN_FIRST)) + list(range(56, 56 + OWN_LAST))):
        h = head_of(slot, y, zh)
        for side in range(2):
            hidden = (query // 128 == side * 2 + h // 4) & (key + side * ROWS + h * UNIT > query)
            hide[(n * 2 + side) * UNIT : (n * 2 + side + 1) * UNIT, :] = jnp.where(hidden, MASKED, 0.0)
    local[0].wait()
    for i in range(HEADS):
        wvt[i * 128 : (i + 1) * 128, :] = wv[:, i * 128 : (i + 1) * 128].T
    local[1].wait()

    for i in range(1, 4):
        unit_in(i).wait_recv()
    share(0, 4, 0, core).start()
    for i in range(4, 8):
        unit_in(i).wait_recv()
    share(4, 4, 8, core).start()
    for i in STAGES[1]:
        pass_unit(i).start()
    for i in (Y2, Z2):
        unit_in(i).wait_recv()
    for i in STAGES[2]:
        pass_unit(i).start()
    for c in swap_in:
        c.wait_recv()
    prepare(theirs)
    share(0, 4, 0, other).wait_recv()
    share(4, 4, 8, other).wait_recv()

    def work(k, first=False, last=False):
        made = {}

        def lanes(a, b):
            return lat[pl.ds(k * 8, 8), :, :, a:b].reshape(CHUNK, b - a)

        def scores(h):
            pair, side = h // 2, h % 2
            if pair not in made:
                cols = slice(pair * 256, (pair + 1) * 256)
                here = lanes(0, LATENT)
                keys = jnp.dot(here, wk[:, cols], preferred_element_type=F32).astype(BF16)
                vals = lax.dot_general(wvt[cols, :], here, NT, preferred_element_type=F32).astype(BF16)
                made[pair] = (keys, vals)
            keys = made[pair][0][:, side * 128 : (side + 1) * 128]
            left = jnp.concatenate([keys, lanes(LATENT, WIDE)], 1)
            right = jnp.concatenate([qn[:, h * 128 : (h + 1) * 128], qrot[h]], 1)
            s = lax.dot_general(left, right, NT, preferred_element_type=F32)
            if first or last:
                start, n = (0, OWN_FIRST * 64) if first else (OWN_FIRST * 64, OWN_LAST * 64)
                s = jnp.concatenate([s[:n] + hide[start : start + n, :], s[n:]], 0)
            return s

        def finish(h, s):
            w = jnp.exp2(s * SCALE2)
            sums = jnp.sum(w.reshape(CHUNK // 8, 8, CHUNK), 0)
            vals = made[h // 2][1][(h % 2) * 128 : (h % 2 + 1) * 128]
            gains = jnp.dot(vals, w.astype(BF16), preferred_element_type=F32)
            if not first:
                sums = total[h] + sums
                gains = acc[h] + gains
            if not last:
                total[h] = sums
                acc[h] = gains
                return None
            row = jnp.sum(sums, 0, keepdims=True)
            done[:, h * 128 : (h + 1) * 128] = (gains / row).T.astype(BF16)
            return row

        held = [scores(h) for h in range(AHEAD)]
        rows_total = []
        for h in range(HEADS):
            if h + AHEAD < HEADS:
                held.append(scores(h + AHEAD))
            rows_total.append(finish(h, held.pop(0)))
        return rows_total

    def keep(k):
        return pltpu.make_async_copy(lat.at[pl.ds(k * 8, 8)], all_hbm.at[pl.ds(k * 8, 8)], all_sem.at[k])

    keep(0).start()
    work(0, first=True)

    def step_body(k, carry):
        @pl.when(k == 1)
        def _():
            for i in range(8):
                unit_in(8 + i).wait_recv()
            share_chunk(1).start()

        for i in range(8):
            if i < 2:
                @pl.when(k < 6)
                def _():
                    unit_in(k * 8 + 8 + i).wait_recv()
            else:
                unit_in(k * 8 + 8 + i).wait_recv()
        share_chunk(k + 1).start()

        @pl.when(k == 1)
        def _():
            for i in STAGES[3]:
                pass_unit(i).start()

        @pl.when(k == 2)
        def _():
            for i in STAGES[4]:
                pass_unit(i).start()

        chunk_in(k).wait_recv()
        keep(k).start()
        work(k)
        return carry

    lax.fori_loop(1, 7, step_body, 0)

    chunk_in(7).wait_recv()
    keep(7).start()
    rows_total = work(7, last=True)

    give = pltpu.make_async_copy(done.at[mine], out_hbm.at[:, mine_cols], o_loc)
    give_away = remote(done.at[theirs], out_hbm.at[:, mine_cols], o_send.at[0], o_recv.at[0], sibling)
    give_away.start()
    give.start()
    most = functools.reduce(jnp.maximum, rows_total)
    least = functools.reduce(jnp.minimum, rows_total)
    for i in range(2):
        here = slice(i * ROWS, (i + 1) * ROWS)
        line = lax.broadcasted_iota(jnp.int32, (8, ROWS), 0)
        peak[i] = jnp.where(line < 4, most[:, here], least[:, here])
    tell = remote(peak.at[other], peak_ref.at[core], o_send.at[1], o_recv.at[1], sibling)
    tell.start()
    peak_ref[core] = peak[core]

    for c in swap:
        c.wait_send()

    def all_sent(i, carry):
        unit_in(i).wait_send()
        return carry

    lax.fori_loop(1, 64, all_sent, 0)
    share(0, 4, 0, core).wait_send()
    share(4, 4, 8, core).wait_send()
    for k in range(1, 8):
        share_chunk(k).wait_send()
    for k in range(8):
        keep(k).wait()
    give.wait()
    give_away.wait_send()
    into = out_hbm.at[:, their_cols]
    remote(into, into, o_send.at[0], o_recv.at[0], sibling).wait_recv()
    tell.wait_send()
    into = peak_ref.at[other]
    remote(into, into, o_send.at[1], o_recv.at[1], sibling).wait_recv()


def settle(
    peak_hbm, pos_ref, fast_hbm, all_hbm, qn_hbm, qr_hbm, wk_hbm, wv_hbm, out_hbm,
    peak, lat, wk, wv, qn, qr, acc, total, top, result, stage, sem, peak_sem, in_sem, out_sem,
):
    through = []
    for i in range(4):
        rows = pl.ds(i * 64, 64)
        through.append(
            (
                pltpu.make_async_copy(fast_hbm.at[rows], stage.at[rows], in_sem.at[i]),
                pltpu.make_async_copy(stage.at[rows], out_hbm.at[rows], out_sem.at[i]),
            )
        )
    for come, _ in through:
        come.start()
    look = pltpu.make_async_copy(peak_hbm, peak, peak_sem)
    look.start()
    for come, go in through:
        come.wait()
        go.start()
    look.wait()
    line = lax.broadcasted_iota(jnp.int32, (2, 8, ROWS), 1)
    low = jnp.where(peak[...] <= 1.0, 1.0, 0.0)
    high = jnp.where(peak[...] >= LEAST, 1.0, 0.0)
    bad = jnp.min(jnp.where(line < 4, low, high)) < 0.5
    for _, go in through:
        go.wait()

    @pl.when(bad)
    def _():
        core = lax.axis_index("seq") % 2
        head = lax.axis_index("head")

        def fetch(src, dst):
            c = pltpu.make_async_copy(src, dst, sem)
            c.start()
            c.wait()

        fetch(all_hbm, lat)
        qmask = query_mask(pos_ref).astype(F32)
        qlane = lax.broadcasted_iota(jnp.int32, (ROWS, 128), 1)

        def one_pair(pair, carry):
            pair_cols = at_rows(pair * 256, 256, 256)
            fetch(wk_hbm.at[:, pair_cols], wk)
            fetch(wv_hbm.at[:, pair_cols], wv)
            fetch(qn_hbm.at[:, pair_cols], qn)
            fetch(qr_hbm.at[:, at_rows(pair * 128, 128, 128)], qr)
            for side in range(2):
                cols = slice(side * 128, (side + 1) * 128)
                both = qr[...].astype(F32)
                if side:
                    both = pltpu.roll(both, ROPE, 1)
                rot = jnp.where(qlane < ROPE, both, qmask).astype(BF16)
                right = jnp.concatenate([qn[:, cols], rot], 1)
                acc[...] = jnp.zeros_like(acc)
                total[...] = jnp.zeros_like(total)
                top[...] = jnp.full_like(top, MASKED)

                def one_block(i, c):
                    rows = lat[pl.ds(i * 4, 4)].reshape(ROWS, WIDE)
                    here = rows[:, :LATENT]
                    keys = jnp.dot(here, wk[:, cols], preferred_element_type=F32).astype(BF16)
                    vals = jnp.dot(here, wv[:, cols], preferred_element_type=F32).astype(BF16)
                    left = jnp.concatenate([keys, rows[:, LATENT:]], 1)
                    s = lax.dot_general(right, left, NT, preferred_element_type=F32)
                    q = lax.broadcasted_iota(jnp.int32, (ROWS, ROWS), 0)
                    k = lax.broadcasted_iota(jnp.int32, (ROWS, ROWS), 1)
                    slot = i * 4 + k // 64
                    h = jnp.full((ROWS, ROWS), 8, jnp.int32)
                    for own in list(range(OWN_FIRST)) + list(range(56, 56 + OWN_LAST)):
                        h = jnp.where(slot == own, head_of(own, head // 2, head % 2), h)
                    own_key = h * UNIT + k % UNIT
                    same = (h < 8) & (k // UNIT % 2 == core) & (own_key // 128 == q // 128)
                    s = jnp.where(same & (own_key > q), MASKED, s) * SCALE2
                    new = jnp.maximum(top[...], jnp.max(s, 1, keepdims=True))
                    w = jnp.where(s > MASKED * SCALE2 / 2, jnp.exp2(s - new[:, :1]), 0.0)
                    factor = jnp.exp2(top[...] - new)
                    total[...] = total[...] * factor + jnp.sum(w, 1, keepdims=True)
                    acc[...] = acc[...] * factor + jnp.dot(w.astype(BF16), vals, preferred_element_type=F32)
                    top[...] = new
                    return c

                lax.fori_loop(0, 16, one_block, 0)
                result[:, cols] = (acc[...] / total[...]).astype(BF16)
            fetch(result, out_hbm.at[:, pair_cols])
            return carry

        lax.fori_loop(0, 8, one_pair, 0)


def per_device(q_nope, q_rope, latent, k_rope, positions, w_uk, w_uv):
    hbm = pl.BlockSpec(memory_space=pltpu.HBM)
    vmem = pl.BlockSpec(memory_space=pltpu.VMEM)
    smem = pl.BlockSpec(memory_space=pltpu.SMEM)
    dma = pltpu.SemaphoreType.DMA
    fast, rows, peak = pl.pallas_call(
        gather_attend,
        out_shape=(
            jax.ShapeDtypeStruct((ROWS, 2 * COLS), BF16),
            jax.ShapeDtypeStruct((64, 2, UNIT, WIDE), BF16),
            jax.ShapeDtypeStruct((2, 8, ROWS), F32),
        ),
        in_specs=[smem, vmem, vmem] + [hbm] * 4,
        out_specs=(hbm, hbm, vmem),
        scratch_shapes=[
            pltpu.VMEM((64, 2, UNIT, WIDE), BF16),
            pltpu.VMEM((LATENT, COLS), BF16),
            pltpu.VMEM((LATENT, COLS), BF16),
            pltpu.VMEM((COLS, LATENT), BF16),
            pltpu.VMEM((CHUNK, COLS), BF16),
            pltpu.VMEM((CHUNK, COLS // 2), BF16),
            pltpu.VMEM((CHUNK, 128), BF16),
            pltpu.VMEM((HEADS, CHUNK, 128), BF16),
            pltpu.VMEM(((OWN_FIRST + OWN_LAST) * 64, CHUNK), F32),
            pltpu.VMEM((HEADS, 128, CHUNK), F32),
            pltpu.VMEM((HEADS, 8, CHUNK), F32),
            pltpu.VMEM((CHUNK, COLS), BF16),
            pltpu.VMEM((2, 8, ROWS), F32),
            dma((4,)),
            dma((3,)), dma((3,)),
            dma((64,)), dma((64,)),
            dma((9,)), dma((9,)),
            dma,
            dma((2,)), dma((2,)),
            dma((8,)),
        ],
        compiler_params=pltpu.CompilerParams(
            collective_id=0, has_side_effects=True, vmem_limit_bytes=56 * 2**20
        ),
        cost_estimate=pl.CostEstimate(flops=26 * 10**9, bytes_accessed=12 * 2**20, transcendentals=17 * 10**6),
        name="gather_attend",
    )(positions, latent, k_rope, q_nope, q_rope, w_uk, w_uv)
    return pl.pallas_call(
        settle,
        out_shape=jax.ShapeDtypeStruct((ROWS, 2 * COLS), BF16),
        in_specs=[hbm, smem] + [hbm] * 6,
        out_specs=hbm,
        scratch_shapes=[
            pltpu.VMEM((2, 8, ROWS), F32),
            pltpu.VMEM((64, 2, UNIT, WIDE), BF16),
            pltpu.VMEM((LATENT, 256), BF16),
            pltpu.VMEM((LATENT, 256), BF16),
            pltpu.VMEM((ROWS, 256), BF16),
            pltpu.VMEM((ROWS, 128), BF16),
            pltpu.VMEM((ROWS, 128), F32),
            pltpu.VMEM((ROWS, 128), F32),
            pltpu.VMEM((ROWS, 128), F32),
            pltpu.VMEM((ROWS, 256), BF16),
            pltpu.VMEM((ROWS, 2 * COLS), BF16),
            dma,
            dma,
            dma((4,)),
            dma((4,)),
        ],
        compiler_params=pltpu.CompilerParams(vmem_limit_bytes=64 * 2**20 - 2**16),
        name="settle",
    )(peak, positions, fast, rows, q_nope, q_rope, w_uk, w_uv)


def solution(mesh):
    in_specs = (
        P("seq", "head"),
        P("seq", "head"),
        P(("seq", "head"), None),
        P(("seq", "head"), None),
        P("seq"),
        P(None, "head"),
        P(None, "head"),
    )
    return jax.shard_map(
        per_device, mesh=mesh, in_specs=in_specs, out_specs=P("seq", "head"), check_vma=False
    )
```

```python
import functools
import math

import jax
import jax.numpy as jnp
from jax import lax
from jax.experimental import pallas as pl
from jax.experimental.pallas import tpu as pltpu
from jax.sharding import PartitionSpec as P

MESH = pl.DeviceIdType.MESH
F32 = jnp.float32
BF16 = jnp.bfloat16
NT = (((1,), (1,)), ((), ()))
NOPE = 128
ROPE = 64
LATENT = 512
WIDE = 640
ROWS = 256
CHUNK = 512
UNIT = 32
HEADS = 8
AHEAD = 3
COLS = HEADS * NOPE
SCALE2 = (NOPE + ROPE) ** (-0.5) * math.log2(math.e)
MASKED = -1e30
SHIFT = 576.0
LEAST = 2.0**-90


def both_signs(pattern):
    found = [()]
    for p in pattern:
        found = [f + (v,) for f in found for v in ((1, 3) if p == 1 else (p,))]
    return found


SLOTS = (
    [(0, 0, 0), (0, 1, 0), (0, 3, 0), (1, 0, 0), (3, 0, 0), (0, 0, 1), (0, 0, 3), (2, 0, 0)]
    + both_signs((1, 1, 0)) + both_signs((1, 0, 1))
    + both_signs((0, 1, 1)) + both_signs((2, 1, 0)) + both_signs((2, 0, 1))
    + both_signs((1, 2, 0)) + both_signs((0, 2, 1)) + both_signs((1, 0, 2)) + [(2, 2, 0), (2, 0, 2)]
    + both_signs((1, 1, 1))
    + both_signs((2, 1, 1)) + both_signs((1, 2, 1))
    + both_signs((1, 1, 2)) + both_signs((2, 2, 1)) + both_signs((1, 2, 2))
    + [(0, 2, 0), (0, 0, 2), (0, 1, 2), (0, 3, 2), (0, 2, 2), (2, 1, 2), (2, 3, 2), (2, 2, 2)]
)
Y2, Z2 = 56, 57
OWN_FIRST, OWN_LAST = 3, 5
STAGES = (
    list(range(1, 8)),
    list(range(8, 24)) + [Y2, Z2],
    list(range(24, 44)) + [58, 59, 60],
    list(range(44, 56)) + [61, 62, 63],
)


def plan_routes():
    place = {s: i for i, s in enumerate(SLOTS)}
    routes = {i: (SLOTS[i], 0) for i in STAGES[0]}
    have = {0}
    for stages, more in zip(STAGES[1:], (STAGES[0], STAGES[1], list(range(24, 40)))):
        have |= set(more)
        load = {}
        options, taken = {}, {}
        for i in stages:
            options[i] = []
            for axis in range(3):
                for way in {0: (), 1: (1,), 3: (3,), 2: (1, 3, 2)}[SLOTS[i][axis]]:
                    step = tuple(way if a == axis else 0 for a in range(3))
                    parent = place[tuple((v - w) % 4 for v, w in zip(SLOTS[i], step))]
                    if parent in have:
                        links = [(axis, w) for w in ((1, 3) if way == 2 else (way,))]
                        options[i].append((step, parent, links))
            single = [o for o in options[i] if len(o[2]) == 1]
            options[i] = single or options[i]
        for i in stages * 6:
            for k in taken.get(i, ((), 0, ()))[2]:
                load[k] -= 1
            taken[i] = min(options[i], key=lambda o: (sum(load.get(k, 0) for k in o[2]) / len(o[2]), o[0], o[1]))
            for k in taken[i][2]:
                load[k] = load.get(k, 0) + 1
        for i in stages:
            routes[i] = taken[i][:2]
    return routes


ROUTES = plan_routes()


def at_rows(start, size, step):
    return pl.ds(pl.multiple_of(start, step), size)


def key_lanes(shape, block):
    return jnp.where(lax.broadcasted_iota(jnp.int32, shape, 1) - ROPE == block, 1.0, 0.0)


def query_mask(pos_ref):
    parts = []
    for i in range(2):
        lane = lax.broadcasted_iota(jnp.int32, (128, 128), 1) - ROPE
        value = jnp.where(lane > pos_ref[i * 128] // 128, MASKED, -SHIFT)
        parts.append(jnp.where((lane >= 0) & (lane < 32), value, 0.0))
    return jnp.concatenate(parts, 0).astype(BF16)


def head_of(slot, y, zh):
    _, dy, dz = SLOTS[slot]
    return ((y + dy) % 4) * 2 + (zh + dz // 2) % 2


def gather_attend(
    pos_ref, lat_ref, rot_ref, qn_hbm, qr_hbm, wk_hbm, wv_hbm,
    fast, all_hbm, peak_ref,
    lat, wk, wv, wvt, qn, qr, qmask, qrot, hide, acc, total, done, peak,
    loc_sem, q_send, q_recv, u_send, u_recv, d_send, d_recv, o_loc, o_send, o_recv, all_sem,
):
    seq = lax.axis_index("seq")
    head = lax.axis_index("head")
    x, zl, core = seq // 4, (seq // 2) % 2, seq % 2
    y, zh = head // 2, head % 2
    z = zh * 2 + zl
    other = 1 - core

    def chip(back):
        px, py, pz = (x + 4 - back[0]) % 4, (y + 4 - back[1]) % 4, (z + 4 - back[2]) % 4
        return (px * 4 + (pz % 2) * 2 + core, py * 2 + pz // 2)

    sibling = (seq + 1 - 2 * core, head)
    partners = [chip(SLOTS[i]) for i in STAGES[0]] + [sibling]

    barrier = pltpu.get_barrier_semaphore()
    for p in partners:
        pl.semaphore_signal(barrier, inc=1, device_id=p, device_id_type=MESH)

    mine = at_rows(core * ROWS, ROWS, ROWS)
    theirs = at_rows(other * ROWS, ROWS, ROWS)
    mine_cols = at_rows(core * COLS, COLS, COLS)
    their_cols = at_rows(other * COLS, COLS, COLS)
    half_cols = COLS // 2
    local = [
        pltpu.make_async_copy(wv_hbm.at[:, mine_cols], wv, loc_sem.at[0]),
        pltpu.make_async_copy(wk_hbm.at[:, mine_cols], wk, loc_sem.at[1]),
        pltpu.make_async_copy(qn_hbm.at[:, mine_cols], qn.at[mine], loc_sem.at[2]),
        pltpu.make_async_copy(
            qr_hbm.at[:, at_rows(core * half_cols, half_cols, half_cols)], qr.at[mine], loc_sem.at[3]
        ),
    ]
    for c in local:
        c.start()

    block = jnp.where(head < 4, pos_ref[0] // 128, pos_ref[128] // 128)
    lane = lax.broadcasted_iota(jnp.int32, (UNIT, 128), 1)
    rot = jnp.concatenate([rot_ref[...].astype(F32), jnp.zeros((UNIT, ROPE), F32)], 1)
    lat[0, core, :, :LATENT] = lat_ref[...]
    lat[0, core, :, LATENT:] = jnp.where(lane < ROPE, rot, key_lanes((UNIT, 128), block)).astype(BF16)
    qmask[mine] = query_mask(pos_ref)

    pl.semaphore_wait(barrier, len(partners))

    def remote(src, dst, send, recv, to):
        return pltpu.make_async_remote_copy(
            src_ref=src, dst_ref=dst, send_sem=send, recv_sem=recv, device_id=to, device_id_type=MESH
        )

    def pass_unit(i):
        step, parent = ROUTES[i]
        return remote(lat.at[parent, core], lat.at[i, core], u_send.at[i], u_recv.at[i], chip(step))

    def unit_in(i):
        ref = lat.at[i, core]
        return remote(ref, ref, u_send.at[i], u_recv.at[i], sibling)

    def share(i, size, sem, side):
        ref = lat.at[pl.ds(i, size), side]
        return remote(ref, ref, d_send.at[sem], d_recv.at[sem], sibling)

    def share_chunk(k):
        return share(k * 8, 8, k, core)

    def chunk_in(k):
        return share(k * 8, 8, k, other)

    for i in STAGES[0]:
        pass_unit(i).start()
    swap = [
        remote(qn_hbm.at[:, their_cols], qn.at[mine], q_send.at[0], q_recv.at[0], sibling),
        remote(
            qr_hbm.at[:, at_rows(other * half_cols, half_cols, half_cols)], qr.at[mine],
            q_send.at[1], q_recv.at[1], sibling,
        ),
        remote(qmask.at[mine], qmask.at[mine], q_send.at[2], q_recv.at[2], sibling),
    ]
    for c in swap:
        c.start()
    swap_in = [
        remote(qn.at[theirs], qn.at[theirs], q_send.at[0], q_recv.at[0], sibling),
        remote(qr.at[theirs], qr.at[theirs], q_send.at[1], q_recv.at[1], sibling),
        remote(qmask.at[theirs], qmask.at[theirs], q_send.at[2], q_recv.at[2], sibling),
    ]

    qlane = lax.broadcasted_iota(jnp.int32, (ROWS, 128), 1)

    def prepare(rows):
        mask_rows = qmask[rows].astype(F32)
        for pair in range(HEADS // 2):
            both = qr[rows, pair * 128 : (pair + 1) * 128].astype(F32)
            qrot[2 * pair, rows] = jnp.where(qlane < ROPE, both, mask_rows).astype(BF16)
            qrot[2 * pair + 1, rows] = jnp.where(qlane < ROPE, pltpu.roll(both, ROPE, 1), mask_rows).astype(BF16)

    local[2].wait()
    local[3].wait()
    prepare(mine)
    key = lax.broadcasted_iota(jnp.int32, (UNIT, CHUNK), 0)
    query = lax.broadcasted_iota(jnp.int32, (UNIT, CHUNK), 1)
    for n, slot in enumerate(list(range(OWN_FIRST)) + list(range(56, 56 + OWN_LAST))):
        h = head_of(slot, y, zh)
        for side in range(2):
            hidden = (query // 128 == side * 2 + h // 4) & (key + side * ROWS + h * UNIT > query)
            hide[(n * 2 + side) * UNIT : (n * 2 + side + 1) * UNIT, :] = jnp.where(hidden, MASKED, 0.0)
    local[0].wait()
    for i in range(HEADS):
        wvt[i * 128 : (i + 1) * 128, :] = wv[:, i * 128 : (i + 1) * 128].T
    local[1].wait()

    for i in range(1, 4):
        unit_in(i).wait_recv()
    share(0, 4, 0, core).start()
    for i in range(4, 8):
        unit_in(i).wait_recv()
    share(4, 4, 8, core).start()
    for i in STAGES[1]:
        pass_unit(i).start()
    for c in swap_in:
        c.wait_recv()
    prepare(theirs)
    share(0, 4, 0, other).wait_recv()
    share(4, 4, 8, other).wait_recv()

    def work(k, side_now=None, first=False, last=False):
        made = {}

        def lanes(a, b):
            if side_now is None:
                return lat[pl.ds(k * 8, 8), :, :, a:b].reshape(CHUNK, b - a)
            return lat[pl.ds(k * 8, 16), side_now, :, a:b].reshape(CHUNK, b - a)

        def scores(h):
            pair, side = h // 2, h % 2
            if pair not in made:
                cols = slice(pair * 256, (pair + 1) * 256)
                here = lanes(0, LATENT)
                keys = jnp.dot(here, wk[:, cols], preferred_element_type=F32).astype(BF16)
                vals = lax.dot_general(wvt[cols, :], here, NT, preferred_element_type=F32).astype(BF16)
                made[pair] = (keys, vals)
            keys = made[pair][0][:, side * 128 : (side + 1) * 128]
            left = jnp.concatenate([keys, lanes(LATENT, WIDE)], 1)
            right = jnp.concatenate([qn[:, h * 128 : (h + 1) * 128], qrot[h]], 1)
            s = lax.dot_general(left, right, NT, preferred_element_type=F32)
            if first or last:
                start, n = (0, OWN_FIRST * 64) if first else (OWN_FIRST * 64, OWN_LAST * 64)
                s = jnp.concatenate([s[:n] + hide[start : start + n, :], s[n:]], 0)
            return s

        def finish(h, s):
            w = jnp.exp2(s * SCALE2)
            sums = jnp.sum(w.reshape(CHUNK // 8, 8, CHUNK), 0)
            vals = made[h // 2][1][(h % 2) * 128 : (h % 2 + 1) * 128]
            gains = jnp.dot(vals, w.astype(BF16), preferred_element_type=F32)
            if not first:
                sums = total[h] + sums
                gains = acc[h] + gains
            if not last:
                total[h] = sums
                acc[h] = gains
                return None
            row = jnp.sum(sums, 0, keepdims=True)
            done[:, h * 128 : (h + 1) * 128] = (gains / row).T.astype(BF16)
            return row

        held = [scores(h) for h in range(AHEAD)]
        rows_total = []
        for h in range(HEADS):
            if h + AHEAD < HEADS:
                held.append(scores(h + AHEAD))
            rows_total.append(finish(h, held.pop(0)))
        return rows_total

    def keep(k):
        return pltpu.make_async_copy(lat.at[pl.ds(k * 8, 8)], all_hbm.at[pl.ds(k * 8, 8)], all_sem.at[k])

    keep(0).start()
    work(0, first=True)

    def arrive(slots):
        for i in slots:
            unit_in(i).wait_recv()

    def step_body(k, carry):
        @pl.when(k == 1)
        def _():
            arrive(list(range(8, 24)) + [Y2, Z2])
            share_chunk(1).start()
            share_chunk(2).start()
            for i in STAGES[2]:
                pass_unit(i).start()

        @pl.when(k == 3)
        def _():
            arrive(range(24, 40))
            share_chunk(3).start()
            share_chunk(4).start()
            for i in STAGES[3]:
                pass_unit(i).start()

        @pl.when(k == 5)
        def _():
            arrive(range(40, 56))
            share_chunk(5).start()
            share_chunk(6).start()

        @pl.when(k == 6)
        def _():
            arrive(range(58, 64))
            share_chunk(7).start()

        @pl.when(k % 2 == 0)
        def _():
            chunk_in(k - 1).wait_recv()
            chunk_in(k).wait_recv()
            keep(k - 1).start()
            keep(k).start()

        late = (k + 1) % 2
        work(k - late, side_now=core + late * (1 - 2 * core))
        return carry

    lax.fori_loop(1, 7, step_body, 0)

    chunk_in(7).wait_recv()
    keep(7).start()
    rows_total = work(7, last=True)

    give = pltpu.make_async_copy(done.at[mine], fast.at[:, mine_cols], o_loc)
    give_away = remote(done.at[theirs], fast.at[:, mine_cols], o_send.at[0], o_recv.at[0], sibling)
    give_away.start()
    give.start()
    most = functools.reduce(jnp.maximum, rows_total)
    least = functools.reduce(jnp.minimum, rows_total)
    for i in range(2):
        here = slice(i * ROWS, (i + 1) * ROWS)
        line = lax.broadcasted_iota(jnp.int32, (8, ROWS), 0)
        peak[i] = jnp.where(line < 4, most[:, here], least[:, here])
    tell = remote(peak.at[other], peak_ref.at[core], o_send.at[1], o_recv.at[1], sibling)
    tell.start()
    peak_ref[core] = peak[core]

    for c in swap:
        c.wait_send()

    def all_sent(i, carry):
        unit_in(i).wait_send()
        return carry

    lax.fori_loop(1, 64, all_sent, 0)
    share(0, 4, 0, core).wait_send()
    share(4, 4, 8, core).wait_send()
    for k in range(1, 8):
        share_chunk(k).wait_send()
    for k in range(8):
        keep(k).wait()
    give.wait()
    give_away.wait_send()
    into = fast.at[:, their_cols]
    remote(into, into, o_send.at[0], o_recv.at[0], sibling).wait_recv()
    tell.wait_send()
    into = peak_ref.at[other]
    remote(into, into, o_send.at[1], o_recv.at[1], sibling).wait_recv()


def settle(
    peak, pos_ref, fast, all_hbm, qn_hbm, qr_hbm, wk_hbm, wv_hbm, out_hbm,
    lat, wk, wv, qn, qr, acc, total, top, result, sem, out_sem,
):
    whole = pltpu.make_async_copy(fast, out_hbm, out_sem)
    whole.start()
    line = lax.broadcasted_iota(jnp.int32, (2, 8, ROWS), 1)
    low = jnp.where(peak[...] <= 1.0, 1.0, 0.0)
    high = jnp.where(peak[...] >= LEAST, 1.0, 0.0)
    bad = jnp.min(jnp.where(line < 4, low, high)) < 0.5
    whole.wait()

    @pl.when(bad)
    def _():
        core = lax.axis_index("seq") % 2
        head = lax.axis_index("head")

        def fetch(src, dst):
            c = pltpu.make_async_copy(src, dst, sem)
            c.start()
            c.wait()

        fetch(all_hbm, lat)
        qmask = query_mask(pos_ref).astype(F32)
        qlane = lax.broadcasted_iota(jnp.int32, (ROWS, 128), 1)

        def one_pair(pair, carry):
            pair_cols = at_rows(pair * 256, 256, 256)
            fetch(wk_hbm.at[:, pair_cols], wk)
            fetch(wv_hbm.at[:, pair_cols], wv)
            fetch(qn_hbm.at[:, pair_cols], qn)
            fetch(qr_hbm.at[:, at_rows(pair * 128, 128, 128)], qr)
            for side in range(2):
                cols = slice(side * 128, (side + 1) * 128)
                both = qr[...].astype(F32)
                if side:
                    both = pltpu.roll(both, ROPE, 1)
                rot = jnp.where(qlane < ROPE, both, qmask).astype(BF16)
                right = jnp.concatenate([qn[:, cols], rot], 1)
                acc[...] = jnp.zeros_like(acc)
                total[...] = jnp.zeros_like(total)
                top[...] = jnp.full_like(top, MASKED)

                def one_block(i, c):
                    rows = lat[pl.ds(i * 4, 4)].reshape(ROWS, WIDE)
                    here = rows[:, :LATENT]
                    keys = jnp.dot(here, wk[:, cols], preferred_element_type=F32).astype(BF16)
                    vals = jnp.dot(here, wv[:, cols], preferred_element_type=F32).astype(BF16)
                    left = jnp.concatenate([keys, rows[:, LATENT:]], 1)
                    s = lax.dot_general(right, left, NT, preferred_element_type=F32)
                    q = lax.broadcasted_iota(jnp.int32, (ROWS, ROWS), 0)
                    k = lax.broadcasted_iota(jnp.int32, (ROWS, ROWS), 1)
                    slot = i * 4 + k // 64
                    h = jnp.full((ROWS, ROWS), 8, jnp.int32)
                    for own in list(range(OWN_FIRST)) + list(range(56, 56 + OWN_LAST)):
                        h = jnp.where(slot == own, head_of(own, head // 2, head % 2), h)
                    own_key = h * UNIT + k % UNIT
                    same = (h < 8) & (k // UNIT % 2 == core) & (own_key // 128 == q // 128)
                    s = jnp.where(same & (own_key > q), MASKED, s) * SCALE2
                    new = jnp.maximum(top[...], jnp.max(s, 1, keepdims=True))
                    w = jnp.where(s > MASKED * SCALE2 / 2, jnp.exp2(s - new[:, :1]), 0.0)
                    factor = jnp.exp2(top[...] - new)
                    total[...] = total[...] * factor + jnp.sum(w, 1, keepdims=True)
                    acc[...] = acc[...] * factor + jnp.dot(w.astype(BF16), vals, preferred_element_type=F32)
                    top[...] = new
                    return c

                lax.fori_loop(0, 16, one_block, 0)
                result[:, cols] = (acc[...] / total[...]).astype(BF16)
            fetch(result, out_hbm.at[:, pair_cols])
            return carry

        lax.fori_loop(0, 8, one_pair, 0)


def per_device(q_nope, q_rope, latent, k_rope, positions, w_uk, w_uv):
    hbm = pl.BlockSpec(memory_space=pltpu.HBM)
    vmem = pl.BlockSpec(memory_space=pltpu.VMEM)
    smem = pl.BlockSpec(memory_space=pltpu.SMEM)
    dma = pltpu.SemaphoreType.DMA
    fast, rows, peak = pl.pallas_call(
        gather_attend,
        out_shape=(
            pltpu.VMEM((ROWS, 2 * COLS), BF16),
            jax.ShapeDtypeStruct((64, 2, UNIT, WIDE), BF16),
            pltpu.VMEM((2, 8, ROWS), F32),
        ),
        in_specs=[smem, vmem, vmem] + [hbm] * 4,
        out_specs=(vmem, hbm, vmem),
        scratch_shapes=[
            pltpu.VMEM((64, 2, UNIT, WIDE), BF16),
            pltpu.VMEM((LATENT, COLS), BF16),
            pltpu.VMEM((LATENT, COLS), BF16),
            pltpu.VMEM((COLS, LATENT), BF16),
            pltpu.VMEM((CHUNK, COLS), BF16),
            pltpu.VMEM((CHUNK, COLS // 2), BF16),
            pltpu.VMEM((CHUNK, 128), BF16),
            pltpu.VMEM((HEADS, CHUNK, 128), BF16),
            pltpu.VMEM(((OWN_FIRST + OWN_LAST) * 64, CHUNK), F32),
            pltpu.VMEM((HEADS, 128, CHUNK), F32),
            pltpu.VMEM((HEADS, 8, CHUNK), F32),
            pltpu.VMEM((CHUNK, COLS), BF16),
            pltpu.VMEM((2, 8, ROWS), F32),
            dma((4,)),
            dma((3,)), dma((3,)),
            dma((64,)), dma((64,)),
            dma((9,)), dma((9,)),
            dma,
            dma((2,)), dma((2,)),
            dma((8,)),
        ],
        compiler_params=pltpu.CompilerParams(
            collective_id=0, has_side_effects=True, vmem_limit_bytes=58 * 2**20
        ),
        cost_estimate=pl.CostEstimate(flops=26 * 10**9, bytes_accessed=12 * 2**20, transcendentals=17 * 10**6),
        name="gather_attend",
    )(positions, latent, k_rope, q_nope, q_rope, w_uk, w_uv)
    fast = pltpu.with_memory_space_constraint(fast, pltpu.VMEM)
    peak = pltpu.with_memory_space_constraint(peak, pltpu.VMEM)
    return pl.pallas_call(
        settle,
        out_shape=jax.ShapeDtypeStruct((ROWS, 2 * COLS), BF16),
        in_specs=[vmem, smem, vmem] + [hbm] * 5,
        out_specs=hbm,
        scratch_shapes=[
            pltpu.VMEM((64, 2, UNIT, WIDE), BF16),
            pltpu.VMEM((LATENT, 256), BF16),
            pltpu.VMEM((LATENT, 256), BF16),
            pltpu.VMEM((ROWS, 256), BF16),
            pltpu.VMEM((ROWS, 128), BF16),
            pltpu.VMEM((ROWS, 128), F32),
            pltpu.VMEM((ROWS, 128), F32),
            pltpu.VMEM((ROWS, 128), F32),
            pltpu.VMEM((ROWS, 256), BF16),
            dma,
            dma,
        ],
        compiler_params=pltpu.CompilerParams(vmem_limit_bytes=59 * 2**20),
        name="settle",
    )(peak, positions, fast, rows, q_nope, q_rope, w_uk, w_uv)


def solution(mesh):
    in_specs = (
        P("seq", "head"),
        P("seq", "head"),
        P(("seq", "head"), None),
        P(("seq", "head"), None),
        P("seq"),
        P(None, "head"),
        P(None, "head"),
    )
    return jax.shard_map(
        per_device, mesh=mesh, in_specs=in_specs, out_specs=P("seq", "head"), check_vma=False
    )
```

```python
import functools
import math

import jax
import jax.numpy as jnp
from jax import lax
from jax.experimental import pallas as pl
from jax.experimental.pallas import tpu as pltpu
from jax.sharding import PartitionSpec as P

MESH = pl.DeviceIdType.MESH
F32 = jnp.float32
BF16 = jnp.bfloat16
NT = (((1,), (1,)), ((), ()))
NOPE = 128
ROPE = 64
LATENT = 512
WIDE = 640
ROWS = 256
CHUNK = 512
UNIT = 32
HEADS = 8
AHEAD = 3
COLS = HEADS * NOPE
SCALE2 = (NOPE + ROPE) ** (-0.5) * math.log2(math.e)
MASKED = -1e30
SHIFT = 576.0
LEAST = 2.0**-90


def both_signs(pattern):
    found = [()]
    for p in pattern:
        found = [f + (v,) for f in found for v in ((1, 3) if p == 1 else (p,))]
    return found


SLOTS = (
    [(0, 0, 0), (0, 1, 0), (0, 3, 0), (1, 0, 0), (3, 0, 0), (0, 0, 1), (0, 0, 3), (2, 0, 0)]
    + both_signs((1, 1, 0)) + [(1, 0, 1), (3, 0, 3), (0, 1, 3), (0, 3, 1)]
    + [(1, 0, 3), (3, 0, 1), (0, 1, 1), (0, 3, 3)] + both_signs((2, 1, 0)) + both_signs((2, 0, 1))
    + both_signs((1, 2, 0)) + both_signs((0, 2, 1)) + both_signs((1, 0, 2)) + [(2, 2, 0), (2, 0, 2)]
    + both_signs((1, 1, 1))
    + both_signs((2, 1, 1)) + both_signs((1, 2, 1))
    + both_signs((1, 1, 2)) + both_signs((2, 2, 1)) + both_signs((1, 2, 2))
    + [(0, 2, 0), (0, 0, 2), (0, 1, 2), (0, 3, 2), (0, 2, 2), (2, 1, 2), (2, 3, 2), (2, 2, 2)]
)
Y2, Z2 = 56, 57
OWN_FIRST, OWN_LAST = 3, 5
STAGES = (
    list(range(1, 8)),
    list(range(8, 24)) + [Y2, Z2],
    list(range(24, 44)) + [58, 59, 60],
    list(range(44, 56)) + [61, 62, 63],
)


def plan_routes():
    place = {s: i for i, s in enumerate(SLOTS)}
    routes = {i: (SLOTS[i], 0) for i in STAGES[0]}
    have = {0}
    for stages, more in zip(STAGES[1:], (STAGES[0], STAGES[1], list(range(24, 40)))):
        have |= set(more)
        load = {}
        options, taken = {}, {}
        for i in stages:
            options[i] = []
            for axis in range(3):
                for way in {0: (), 1: (1,), 3: (3,), 2: (1, 3, 2)}[SLOTS[i][axis]]:
                    step = tuple(way if a == axis else 0 for a in range(3))
                    parent = place[tuple((v - w) % 4 for v, w in zip(SLOTS[i], step))]
                    if parent in have:
                        links = [(axis, w) for w in ((1, 3) if way == 2 else (way,))]
                        options[i].append((step, parent, links))
            single = [o for o in options[i] if len(o[2]) == 1]
            options[i] = single or options[i]
        for i in stages * 6:
            for k in taken.get(i, ((), 0, ()))[2]:
                load[k] -= 1
            taken[i] = min(options[i], key=lambda o: (sum(load.get(k, 0) for k in o[2]) / len(o[2]), o[0], o[1]))
            for k in taken[i][2]:
                load[k] = load.get(k, 0) + 1
        for i in stages:
            routes[i] = taken[i][:2]
    return routes


ROUTES = plan_routes()


def at_rows(start, size, step):
    return pl.ds(pl.multiple_of(start, step), size)


def key_lanes(shape, block):
    return jnp.where(lax.broadcasted_iota(jnp.int32, shape, 1) - ROPE == block, 1.0, 0.0)


def query_mask(pos_ref):
    parts = []
    for i in range(2):
        lane = lax.broadcasted_iota(jnp.int32, (128, 128), 1) - ROPE
        value = jnp.where(lane > pos_ref[i * 128] // 128, MASKED, -SHIFT)
        parts.append(jnp.where((lane >= 0) & (lane < 32), value, 0.0))
    return jnp.concatenate(parts, 0).astype(BF16)


def head_of(slot, y, zh):
    _, dy, dz = SLOTS[slot]
    return ((y + dy) % 4) * 2 + (zh + dz // 2) % 2


def gather_attend(
    pos_ref, lat_ref, rot_ref, qn_hbm, qr_hbm, wk_hbm, wv_hbm,
    fast, all_hbm, peak_ref,
    lat, wk, wv, wvt, qn, qr, qmask, qrot, hide, acc, total, done, peak,
    loc_sem, q_send, q_recv, u_send, u_recv, d_send, d_recv, o_loc, o_send, o_recv, all_sem,
):
    seq = lax.axis_index("seq")
    head = lax.axis_index("head")
    x, zl, core = seq // 4, (seq // 2) % 2, seq % 2
    y, zh = head // 2, head % 2
    z = zh * 2 + zl
    other = 1 - core

    def chip(back):
        px, py, pz = (x + 4 - back[0]) % 4, (y + 4 - back[1]) % 4, (z + 4 - back[2]) % 4
        return (px * 4 + (pz % 2) * 2 + core, py * 2 + pz // 2)

    sibling = (seq + 1 - 2 * core, head)
    near = STAGES[0] + [Y2, Z2]
    partners = [chip(SLOTS[i]) for i in near] + [sibling]

    barrier = pltpu.get_barrier_semaphore()
    for p in partners:
        pl.semaphore_signal(barrier, inc=1, device_id=p, device_id_type=MESH)

    theirs, mine = pl.ds(0, ROWS), pl.ds(ROWS, ROWS)
    mine_cols = at_rows(core * COLS, COLS, COLS)
    their_cols = at_rows(other * COLS, COLS, COLS)
    half_cols = COLS // 2
    local = [
        pltpu.make_async_copy(wv_hbm.at[:, mine_cols], wv, loc_sem.at[0]),
        pltpu.make_async_copy(wk_hbm.at[:, mine_cols], wk, loc_sem.at[1]),
        pltpu.make_async_copy(qn_hbm.at[:, mine_cols], qn.at[mine], loc_sem.at[2]),
        pltpu.make_async_copy(
            qr_hbm.at[:, at_rows(core * half_cols, half_cols, half_cols)], qr.at[mine], loc_sem.at[3]
        ),
    ]
    for c in local:
        c.start()

    block = jnp.where(head < 4, pos_ref[0] // 128, pos_ref[128] // 128)
    lane = lax.broadcasted_iota(jnp.int32, (UNIT, 128), 1)
    rot = jnp.concatenate([rot_ref[...].astype(F32), jnp.zeros((UNIT, ROPE), F32)], 1)
    lat[0, core, :, :LATENT] = lat_ref[...]
    lat[0, core, :, LATENT:] = jnp.where(lane < ROPE, rot, key_lanes((UNIT, 128), block)).astype(BF16)
    qmask[mine] = query_mask(pos_ref)

    pl.semaphore_wait(barrier, len(partners))

    def remote(src, dst, send, recv, to):
        return pltpu.make_async_remote_copy(
            src_ref=src, dst_ref=dst, send_sem=send, recv_sem=recv, device_id=to, device_id_type=MESH
        )

    def pass_unit(i):
        step, parent = ROUTES[i]
        return remote(lat.at[parent, core], lat.at[i, core], u_send.at[i], u_recv.at[i], chip(step))

    def unit_in(i):
        ref = lat.at[i, core]
        return remote(ref, ref, u_send.at[i], u_recv.at[i], sibling)

    def share(i, size, sem, side):
        ref = lat.at[pl.ds(i, size), side]
        return remote(ref, ref, d_send.at[sem], d_recv.at[sem], sibling)

    def share_chunk(k):
        return share(k * 8, 8, k, core)

    def chunk_in(k):
        return share(k * 8, 8, k, other)

    for i in STAGES[0]:
        pass_unit(i).start()
    swap = [
        remote(qn_hbm.at[:, their_cols], qn.at[theirs], q_send.at[0], q_recv.at[0], sibling),
        remote(
            qr_hbm.at[:, at_rows(other * half_cols, half_cols, half_cols)], qr.at[theirs],
            q_send.at[1], q_recv.at[1], sibling,
        ),
        remote(qmask.at[mine], qmask.at[theirs], q_send.at[2], q_recv.at[2], sibling),
    ]
    for c in swap:
        c.start()
    swap_in = [
        remote(qn.at[theirs], qn.at[theirs], q_send.at[0], q_recv.at[0], sibling),
        remote(qr.at[theirs], qr.at[theirs], q_send.at[1], q_recv.at[1], sibling),
        remote(qmask.at[theirs], qmask.at[theirs], q_send.at[2], q_recv.at[2], sibling),
    ]

    qlane = lax.broadcasted_iota(jnp.int32, (ROWS, 128), 1)

    def prepare(rows):
        mask_rows = qmask[rows].astype(F32)
        for pair in range(HEADS // 2):
            both = qr[rows, pair * 128 : (pair + 1) * 128].astype(F32)
            qrot[2 * pair, rows] = jnp.where(qlane < ROPE, both, mask_rows).astype(BF16)
            qrot[2 * pair + 1, rows] = jnp.where(qlane < ROPE, pltpu.roll(both, ROPE, 1), mask_rows).astype(BF16)

    local[2].wait()
    local[3].wait()
    prepare(mine)
    key = lax.broadcasted_iota(jnp.int32, (UNIT, CHUNK), 0)
    query = lax.broadcasted_iota(jnp.int32, (UNIT, CHUNK), 1)
    query = query + jnp.where(query < ROWS, other * ROWS, (core - 1) * ROWS)
    for n, slot in enumerate(list(range(OWN_FIRST)) + list(range(56, 56 + OWN_LAST))):
        h = head_of(slot, y, zh)
        for side in range(2):
            hidden = (query // 128 == side * 2 + h // 4) & (key + side * ROWS + h * UNIT > query)
            hide[(n * 2 + side) * UNIT : (n * 2 + side + 1) * UNIT, :] = jnp.where(hidden, MASKED, 0.0)
    local[0].wait()
    for i in range(HEADS):
        wvt[i * 128 : (i + 1) * 128, :] = wv[:, i * 128 : (i + 1) * 128].T
    local[1].wait()
    for c in swap_in:
        c.wait_recv()
    prepare(theirs)

    for i in range(1, 4):
        unit_in(i).wait_recv()
    share(0, 4, 0, core).start()
    for i in range(4, 8):
        unit_in(i).wait_recv()
    share(4, 4, 8, core).start()
    for i in STAGES[1]:
        pass_unit(i).start()
    share(0, 4, 0, other).wait_recv()
    share(4, 4, 8, other).wait_recv()

    def work(k, side_now=None, first=False, last=False):
        made = {}

        def lanes(a, b):
            if side_now is None:
                return lat[pl.ds(k * 8, 8), :, :, a:b].reshape(CHUNK, b - a)
            return lat[pl.ds(k * 8, 16), side_now, :, a:b].reshape(CHUNK, b - a)

        def scores(h, at):
            pair, side = h // 2, h % 2
            if pair not in made:
                cols = slice(pair * 256, (pair + 1) * 256)
                here = lanes(0, LATENT)
                keys = jnp.dot(here, wk[:, cols], preferred_element_type=F32).astype(BF16)
                vals = lax.dot_general(wvt[cols, :], here, NT, preferred_element_type=F32).astype(BF16)
                made[pair] = (keys, vals)
            keys = made[pair][0][:, side * 128 : (side + 1) * 128]
            left = jnp.concatenate([keys, lanes(LATENT, WIDE)], 1)
            right = jnp.concatenate([qn[at, h * 128 : (h + 1) * 128], qrot[h, at]], 1)
            s = lax.dot_general(left, right, NT, preferred_element_type=F32)
            if first or last:
                start, n = (0, OWN_FIRST * 64) if first else (OWN_FIRST * 64, OWN_LAST * 64)
                s = jnp.concatenate([s[:n] + hide[start : start + n, at], s[n:]], 0)
            return s

        def finish(h, at, s):
            w = jnp.exp2(s * SCALE2)
            sums = jnp.sum(w.reshape(CHUNK // 8, 8, at.stop - at.start), 0)
            vals = made[h // 2][1][(h % 2) * 128 : (h % 2 + 1) * 128]
            gains = jnp.dot(vals, w.astype(BF16), preferred_element_type=F32)
            if not first:
                sums = total[h, :, at] + sums
                gains = acc[h, :, at] + gains
            if not last:
                total[h, :, at] = sums
                acc[h, :, at] = gains
                return None
            row = jnp.sum(sums, 0, keepdims=True)
            done[at, h * 128 : (h + 1) * 128] = (gains / row).T.astype(BF16)
            return row

        def sweep(at, ahead):
            held = [scores(h, at) for h in range(ahead)]
            rows_total = []
            for h in range(HEADS):
                if h + ahead < HEADS:
                    held.append(scores(h + ahead, at))
                rows_total.append(finish(h, at, held.pop(0)))
            return rows_total

        if not last:
            sweep(slice(0, CHUNK), AHEAD)
            return
        for half in range(2):
            rows_total = sweep(slice(half * ROWS, (half + 1) * ROWS), 2 * AHEAD - 1)
            most = functools.reduce(jnp.maximum, rows_total)
            least = functools.reduce(jnp.minimum, rows_total)
            line = lax.broadcasted_iota(jnp.int32, (8, ROWS), 0)
            both = jnp.where(line < 4, most, least)
            if half:
                peak_ref[0] = both
                give.start()
            else:
                peak[...] = both
                give_away.start()
                tell.start()

    give = pltpu.make_async_copy(done.at[mine], fast.at[:, mine_cols], o_loc)
    give_away = remote(done.at[theirs], fast.at[:, mine_cols], o_send.at[0], o_recv.at[0], sibling)
    tell = remote(peak, peak_ref.at[1], o_send.at[1], o_recv.at[1], sibling)

    def keep(k):
        return pltpu.make_async_copy(lat.at[pl.ds(k * 8, 8)], all_hbm.at[pl.ds(k * 8, 8)], all_sem.at[k])

    keep(0).start()
    work(0, first=True)

    def arrive(slots):
        for i in slots:
            unit_in(i).wait_recv()

    def step_body(k, carry):
        @pl.when(k == 1)
        def _():
            arrive(list(range(8, 24)) + [Y2, Z2])
            share_chunk(1).start()
            share_chunk(2).start()
            for i in STAGES[2]:
                pass_unit(i).start()

        @pl.when(k == 3)
        def _():
            arrive(range(24, 40))
            share_chunk(3).start()
            share_chunk(4).start()
            for i in STAGES[3]:
                pass_unit(i).start()

        @pl.when(k == 5)
        def _():
            arrive(range(40, 56))
            share_chunk(5).start()
            share_chunk(6).start()

        @pl.when(k == 6)
        def _():
            arrive(range(58, 64))
            share_chunk(7).start()

        @pl.when(k % 2 == 0)
        def _():
            chunk_in(k - 1).wait_recv()
            chunk_in(k).wait_recv()
            keep(k - 1).start()
            keep(k).start()

        late = (k + 1) % 2
        work(k - late, side_now=core + late * (1 - 2 * core))
        return carry

    lax.fori_loop(1, 7, step_body, 0)

    chunk_in(7).wait_recv()
    keep(7).start()
    work(7, last=True)

    for c in swap:
        c.wait_send()

    def all_sent(i, carry):
        unit_in(i).wait_send()
        return carry

    lax.fori_loop(1, 64, all_sent, 0)
    share(0, 4, 0, core).wait_send()
    share(4, 4, 8, core).wait_send()
    for k in range(1, 8):
        share_chunk(k).wait_send()
    for k in range(8):
        keep(k).wait()
    give.wait()
    give_away.wait_send()
    into = fast.at[:, their_cols]
    remote(into, into, o_send.at[0], o_recv.at[0], sibling).wait_recv()
    tell.wait()


def settle(
    peak, pos_ref, fast, all_hbm, qn_hbm, qr_hbm, wk_hbm, wv_hbm, out_hbm,
    lat, wk, wv, qn, qr, acc, total, top, result, sem, out_sem,
):
    whole = pltpu.make_async_copy(fast, out_hbm, out_sem)
    whole.start()
    line = lax.broadcasted_iota(jnp.int32, (2, 8, ROWS), 1)
    low = jnp.where(peak[...] <= 1.0, 1.0, 0.0)
    high = jnp.where(peak[...] >= LEAST, 1.0, 0.0)
    bad = jnp.min(jnp.where(line < 4, low, high)) < 0.5
    whole.wait()

    @pl.when(bad)
    def _():
        core = lax.axis_index("seq") % 2
        head = lax.axis_index("head")

        def fetch(src, dst):
            c = pltpu.make_async_copy(src, dst, sem)
            c.start()
            c.wait()

        fetch(all_hbm, lat)
        qmask = query_mask(pos_ref).astype(F32)
        qlane = lax.broadcasted_iota(jnp.int32, (ROWS, 128), 1)

        def one_pair(pair, carry):
            pair_cols = at_rows(pair * 256, 256, 256)
            fetch(wk_hbm.at[:, pair_cols], wk)
            fetch(wv_hbm.at[:, pair_cols], wv)
            fetch(qn_hbm.at[:, pair_cols], qn)
            fetch(qr_hbm.at[:, at_rows(pair * 128, 128, 128)], qr)
            for side in range(2):
                cols = slice(side * 128, (side + 1) * 128)
                both = qr[...].astype(F32)
                if side:
                    both = pltpu.roll(both, ROPE, 1)
                rot = jnp.where(qlane < ROPE, both, qmask).astype(BF16)
                right = jnp.concatenate([qn[:, cols], rot], 1)
                acc[...] = jnp.zeros_like(acc)
                total[...] = jnp.zeros_like(total)
                top[...] = jnp.full_like(top, MASKED)

                def one_block(i, c):
                    rows = lat[pl.ds(i * 4, 4)].reshape(ROWS, WIDE)
                    here = rows[:, :LATENT]
                    keys = jnp.dot(here, wk[:, cols], preferred_element_type=F32).astype(BF16)
                    vals = jnp.dot(here, wv[:, cols], preferred_element_type=F32).astype(BF16)
                    left = jnp.concatenate([keys, rows[:, LATENT:]], 1)
                    s = lax.dot_general(right, left, NT, preferred_element_type=F32)
                    q = lax.broadcasted_iota(jnp.int32, (ROWS, ROWS), 0)
                    k = lax.broadcasted_iota(jnp.int32, (ROWS, ROWS), 1)
                    slot = i * 4 + k // 64
                    h = jnp.full((ROWS, ROWS), 8, jnp.int32)
                    for own in list(range(OWN_FIRST)) + list(range(56, 56 + OWN_LAST)):
                        h = jnp.where(slot == own, head_of(own, head // 2, head % 2), h)
                    own_key = h * UNIT + k % UNIT
                    same = (h < 8) & (k // UNIT % 2 == core) & (own_key // 128 == q // 128)
                    s = jnp.where(same & (own_key > q), MASKED, s) * SCALE2
                    new = jnp.maximum(top[...], jnp.max(s, 1, keepdims=True))
                    w = jnp.where(s > MASKED * SCALE2 / 2, jnp.exp2(s - new[:, :1]), 0.0)
                    factor = jnp.exp2(top[...] - new)
                    total[...] = total[...] * factor + jnp.sum(w, 1, keepdims=True)
                    acc[...] = acc[...] * factor + jnp.dot(w.astype(BF16), vals, preferred_element_type=F32)
                    top[...] = new
                    return c

                lax.fori_loop(0, 16, one_block, 0)
                result[:, cols] = (acc[...] / total[...]).astype(BF16)
            fetch(result, out_hbm.at[:, pair_cols])
            return carry

        lax.fori_loop(0, 8, one_pair, 0)


def per_device(q_nope, q_rope, latent, k_rope, positions, w_uk, w_uv):
    hbm = pl.BlockSpec(memory_space=pltpu.HBM)
    vmem = pl.BlockSpec(memory_space=pltpu.VMEM)
    smem = pl.BlockSpec(memory_space=pltpu.SMEM)
    dma = pltpu.SemaphoreType.DMA
    fast, rows, peak = pl.pallas_call(
        gather_attend,
        out_shape=(
            pltpu.VMEM((ROWS, 2 * COLS), BF16),
            jax.ShapeDtypeStruct((64, 2, UNIT, WIDE), BF16),
            pltpu.VMEM((2, 8, ROWS), F32),
        ),
        in_specs=[smem, vmem, vmem] + [hbm] * 4,
        out_specs=(vmem, hbm, vmem),
        scratch_shapes=[
            pltpu.VMEM((64, 2, UNIT, WIDE), BF16),
            pltpu.VMEM((LATENT, COLS), BF16),
            pltpu.VMEM((LATENT, COLS), BF16),
            pltpu.VMEM((COLS, LATENT), BF16),
            pltpu.VMEM((CHUNK, COLS), BF16),
            pltpu.VMEM((CHUNK, COLS // 2), BF16),
            pltpu.VMEM((CHUNK, 128), BF16),
            pltpu.VMEM((HEADS, CHUNK, 128), BF16),
            pltpu.VMEM(((OWN_FIRST + OWN_LAST) * 64, CHUNK), F32),
            pltpu.VMEM((HEADS, 128, CHUNK), F32),
            pltpu.VMEM((HEADS, 8, CHUNK), F32),
            pltpu.VMEM((CHUNK, COLS), BF16),
            pltpu.VMEM((8, ROWS), F32),
            dma((4,)),
            dma((3,)), dma((3,)),
            dma((64,)), dma((64,)),
            dma((9,)), dma((9,)),
            dma,
            dma((2,)), dma((2,)),
            dma((8,)),
        ],
        compiler_params=pltpu.CompilerParams(
            collective_id=0, has_side_effects=True, vmem_limit_bytes=58 * 2**20
        ),
        cost_estimate=pl.CostEstimate(flops=26 * 10**9, bytes_accessed=12 * 2**20, transcendentals=17 * 10**6),
        name="gather_attend",
    )(positions, latent, k_rope, q_nope, q_rope, w_uk, w_uv)
    fast = pltpu.with_memory_space_constraint(fast, pltpu.VMEM)
    peak = pltpu.with_memory_space_constraint(peak, pltpu.VMEM)
    return pl.pallas_call(
        settle,
        out_shape=jax.ShapeDtypeStruct((ROWS, 2 * COLS), BF16),
        in_specs=[vmem, smem, vmem] + [hbm] * 5,
        out_specs=hbm,
        scratch_shapes=[
            pltpu.VMEM((64, 2, UNIT, WIDE), BF16),
            pltpu.VMEM((LATENT, 256), BF16),
            pltpu.VMEM((LATENT, 256), BF16),
            pltpu.VMEM((ROWS, 256), BF16),
            pltpu.VMEM((ROWS, 128), BF16),
            pltpu.VMEM((ROWS, 128), F32),
            pltpu.VMEM((ROWS, 128), F32),
            pltpu.VMEM((ROWS, 128), F32),
            pltpu.VMEM((ROWS, 256), BF16),
            dma,
            dma,
        ],
        compiler_params=pltpu.CompilerParams(vmem_limit_bytes=59 * 2**20),
        name="settle",
    )(peak, positions, fast, rows, q_nope, q_rope, w_uk, w_uv)


def solution(mesh):
    in_specs = (
        P("seq", "head"),
        P("seq", "head"),
        P(("seq", "head"), None),
        P(("seq", "head"), None),
        P("seq"),
        P(None, "head"),
        P(None, "head"),
    )
    return jax.shard_map(
        per_device, mesh=mesh, in_specs=in_specs, out_specs=P("seq", "head"), check_vma=False
    )
```

```python
import functools
import math

import jax
import jax.numpy as jnp
from jax import lax
from jax.experimental import pallas as pl
from jax.experimental.pallas import tpu as pltpu
from jax.sharding import PartitionSpec as P

MESH = pl.DeviceIdType.MESH
F32 = jnp.float32
BF16 = jnp.bfloat16
NT = (((1,), (1,)), ((), ()))
NOPE = 128
ROPE = 64
LATENT = 512
WIDE = 640
ROWS = 256
CHUNK = 512
UNIT = 32
HEADS = 8
AHEAD = 3
COLS = HEADS * NOPE
SCALE2 = (NOPE + ROPE) ** (-0.5) * math.log2(math.e)
MASKED = -1e30
SHIFT = 576.0
LEAST = 2.0**-90


def both_signs(pattern):
    found = [()]
    for p in pattern:
        found = [f + (v,) for f in found for v in ((1, 3) if p == 1 else (p,))]
    return found


SLOTS = (
    [(0, 0, 0), (0, 1, 0), (0, 3, 0), (1, 0, 0), (3, 0, 0), (0, 0, 1), (0, 0, 3), (2, 0, 0)]
    + both_signs((1, 1, 0)) + [(1, 0, 1), (3, 0, 3), (0, 1, 3), (0, 3, 1)]
    + [(1, 0, 3), (3, 0, 1), (0, 1, 1), (0, 3, 3)] + both_signs((2, 1, 0)) + both_signs((2, 0, 1))
    + both_signs((1, 2, 0)) + both_signs((0, 2, 1)) + both_signs((1, 0, 2)) + [(2, 2, 0), (2, 0, 2)]
    + both_signs((1, 1, 1))
    + both_signs((2, 1, 1)) + both_signs((1, 2, 1))
    + both_signs((1, 1, 2)) + both_signs((2, 2, 1)) + both_signs((1, 2, 2))
    + [(0, 2, 0), (0, 0, 2), (0, 1, 2), (0, 3, 2), (0, 2, 2), (2, 1, 2), (2, 3, 2), (2, 2, 2)]
)
Y2, Z2 = 56, 57
OWN_FIRST, OWN_LAST = 3, 5
STAGES = (
    list(range(1, 8)) + [Y2, Z2],
    list(range(8, 24)),
    list(range(24, 44)) + [58, 59, 60],
    list(range(44, 56)) + [61, 62, 63],
)


def plan_routes():
    place = {s: i for i, s in enumerate(SLOTS)}
    routes = {i: (SLOTS[i], 0) for i in STAGES[0]}
    have = {0}
    for stages, more in zip(STAGES[1:], (STAGES[0][:7], STAGES[1] + [Y2, Z2], list(range(24, 40)))):
        have |= set(more)
        load = {}
        options, taken = {}, {}
        for i in stages:
            options[i] = []
            for axis in range(3):
                for way in {0: (), 1: (1,), 3: (3,), 2: (1, 3, 2)}[SLOTS[i][axis]]:
                    step = tuple(way if a == axis else 0 for a in range(3))
                    parent = place[tuple((v - w) % 4 for v, w in zip(SLOTS[i], step))]
                    if parent in have:
                        links = [(axis, w) for w in ((1, 3) if way == 2 else (way,))]
                        options[i].append((step, parent, links))
            single = [o for o in options[i] if len(o[2]) == 1]
            options[i] = single or options[i]
        for i in stages * 6:
            for k in taken.get(i, ((), 0, ()))[2]:
                load[k] -= 1
            taken[i] = min(options[i], key=lambda o: (sum(load.get(k, 0) for k in o[2]) / len(o[2]), o[0], o[1]))
            for k in taken[i][2]:
                load[k] = load.get(k, 0) + 1
        for i in stages:
            routes[i] = taken[i][:2]
    return routes


ROUTES = plan_routes()
FIRST_SHARES = ((0, 4, 0), (4, 3, 8), (7, 1, 9))


def at_rows(start, size, step):
    return pl.ds(pl.multiple_of(start, step), size)


def key_lanes(shape, block):
    return jnp.where(lax.broadcasted_iota(jnp.int32, shape, 1) - ROPE == block, 1.0, 0.0)


def query_mask(pos_ref):
    parts = []
    for i in range(2):
        lane = lax.broadcasted_iota(jnp.int32, (128, 128), 1) - ROPE
        value = jnp.where(lane > pos_ref[i * 128] // 128, MASKED, -SHIFT)
        parts.append(jnp.where((lane >= 0) & (lane < 32), value, 0.0))
    return jnp.concatenate(parts, 0).astype(BF16)


def head_of(slot, y, zh):
    _, dy, dz = SLOTS[slot]
    return ((y + dy) % 4) * 2 + (zh + dz // 2) % 2


def gather_attend(
    pos_ref, lat_ref, rot_ref, qn_hbm, qr_hbm, wk_hbm, wv_hbm,
    fast, all_hbm, peak_ref,
    lat, wk, wv, wvt, qn, qr, qmask, qrot, hide, acc, total, done, peak,
    loc_sem, q_send, q_recv, u_send, u_recv, d_send, d_recv, o_loc, o_send, o_recv, all_sem,
):
    seq = lax.axis_index("seq")
    head = lax.axis_index("head")
    x, zl, core = seq // 4, (seq // 2) % 2, seq % 2
    y, zh = head // 2, head % 2
    z = zh * 2 + zl
    other = 1 - core

    def chip(back):
        px, py, pz = (x + 4 - back[0]) % 4, (y + 4 - back[1]) % 4, (z + 4 - back[2]) % 4
        return (px * 4 + (pz % 2) * 2 + core, py * 2 + pz // 2)

    sibling = (seq + 1 - 2 * core, head)
    near = STAGES[0]
    partners = [chip(SLOTS[i]) for i in near] + [sibling]

    barrier = pltpu.get_barrier_semaphore()
    for p in partners:
        pl.semaphore_signal(barrier, inc=1, device_id=p, device_id_type=MESH)

    theirs, mine = pl.ds(0, ROWS), pl.ds(ROWS, ROWS)
    mine_cols = at_rows(core * COLS, COLS, COLS)
    their_cols = at_rows(other * COLS, COLS, COLS)
    half_cols = COLS // 2
    local = [
        pltpu.make_async_copy(wv_hbm.at[:, mine_cols], wv, loc_sem.at[0]),
        pltpu.make_async_copy(wk_hbm.at[:, mine_cols], wk, loc_sem.at[1]),
        pltpu.make_async_copy(qn_hbm.at[:, mine_cols], qn.at[mine], loc_sem.at[2]),
        pltpu.make_async_copy(
            qr_hbm.at[:, at_rows(core * half_cols, half_cols, half_cols)], qr.at[mine], loc_sem.at[3]
        ),
    ]
    for c in local:
        c.start()

    block = jnp.where(head < 4, pos_ref[0] // 128, pos_ref[128] // 128)
    lane = lax.broadcasted_iota(jnp.int32, (UNIT, 128), 1)
    rot = jnp.concatenate([rot_ref[...].astype(F32), jnp.zeros((UNIT, ROPE), F32)], 1)
    lat[0, core, :, :LATENT] = lat_ref[...]
    lat[0, core, :, LATENT:] = jnp.where(lane < ROPE, rot, key_lanes((UNIT, 128), block)).astype(BF16)
    qmask[mine] = query_mask(pos_ref)

    pl.semaphore_wait(barrier, len(partners))

    def remote(src, dst, send, recv, to):
        return pltpu.make_async_remote_copy(
            src_ref=src, dst_ref=dst, send_sem=send, recv_sem=recv, device_id=to, device_id_type=MESH
        )

    def pass_unit(i):
        step, parent = ROUTES[i]
        return remote(lat.at[parent, core], lat.at[i, core], u_send.at[i], u_recv.at[i], chip(step))

    def unit_in(i):
        ref = lat.at[i, core]
        return remote(ref, ref, u_send.at[i], u_recv.at[i], sibling)

    def share(i, size, sem, side):
        ref = lat.at[pl.ds(i, size), side]
        return remote(ref, ref, d_send.at[sem], d_recv.at[sem], sibling)

    def share_chunk(k):
        return share(k * 8, 8, k, core)

    def chunk_in(k):
        return share(k * 8, 8, k, other)

    for i in STAGES[0]:
        pass_unit(i).start()
    swap = [
        remote(qn_hbm.at[:, their_cols], qn.at[theirs], q_send.at[0], q_recv.at[0], sibling),
        remote(
            qr_hbm.at[:, at_rows(other * half_cols, half_cols, half_cols)], qr.at[theirs],
            q_send.at[1], q_recv.at[1], sibling,
        ),
        remote(qmask.at[mine], qmask.at[theirs], q_send.at[2], q_recv.at[2], sibling),
    ]
    for c in swap:
        c.start()
    swap_in = [
        remote(qn.at[theirs], qn.at[theirs], q_send.at[0], q_recv.at[0], sibling),
        remote(qr.at[theirs], qr.at[theirs], q_send.at[1], q_recv.at[1], sibling),
        remote(qmask.at[theirs], qmask.at[theirs], q_send.at[2], q_recv.at[2], sibling),
    ]

    qlane = lax.broadcasted_iota(jnp.int32, (ROWS, 128), 1)

    def prepare(rows):
        mask_rows = qmask[rows].astype(F32)
        for pair in range(HEADS // 2):
            both = qr[rows, pair * 128 : (pair + 1) * 128].astype(F32)
            qrot[2 * pair, rows] = jnp.where(qlane < ROPE, both, mask_rows).astype(BF16)
            qrot[2 * pair + 1, rows] = jnp.where(qlane < ROPE, pltpu.roll(both, ROPE, 1), mask_rows).astype(BF16)

    local[2].wait()
    local[3].wait()
    prepare(mine)
    key = lax.broadcasted_iota(jnp.int32, (UNIT, CHUNK), 0)
    query = lax.broadcasted_iota(jnp.int32, (UNIT, CHUNK), 1)
    query = query + jnp.where(query < ROWS, other * ROWS, (core - 1) * ROWS)
    for n, slot in enumerate(list(range(OWN_FIRST)) + list(range(56, 56 + OWN_LAST))):
        h = head_of(slot, y, zh)
        for side in range(2):
            hidden = (query // 128 == side * 2 + h // 4) & (key + side * ROWS + h * UNIT > query)
            hide[(n * 2 + side) * UNIT : (n * 2 + side + 1) * UNIT, :] = jnp.where(hidden, MASKED, 0.0)
    local[0].wait()
    for i in range(HEADS):
        wvt[i * 128 : (i + 1) * 128, :] = wv[:, i * 128 : (i + 1) * 128].T
    local[1].wait()
    for c in swap_in:
        c.wait_recv()
    prepare(theirs)

    for i in STAGES[0][:7]:
        unit_in(i).wait_recv()
        for j in STAGES[1]:
            if ROUTES[j][1] == i:
                pass_unit(j).start()
        for part in FIRST_SHARES:
            if part[0] + part[1] == i + 1:
                share(*part, core).start()
    for part in FIRST_SHARES:
        share(*part, other).wait_recv()

    def work(k, side_now=None, first=False, last=False):
        made = {}

        def lanes(a, b):
            if side_now is None:
                return lat[pl.ds(k * 8, 8), :, :, a:b].reshape(CHUNK, b - a)
            return lat[pl.ds(k * 8, 16), side_now, :, a:b].reshape(CHUNK, b - a)

        def scores(h, at):
            pair, side = h // 2, h % 2
            if pair not in made:
                cols = slice(pair * 256, (pair + 1) * 256)
                here = lanes(0, LATENT)
                keys = jnp.dot(here, wk[:, cols], preferred_element_type=F32).astype(BF16)
                vals = lax.dot_general(wvt[cols, :], here, NT, preferred_element_type=F32).astype(BF16)
                made[pair] = (keys, vals)
            keys = made[pair][0][:, side * 128 : (side + 1) * 128]
            left = jnp.concatenate([keys, lanes(LATENT, WIDE)], 1)
            right = jnp.concatenate([qn[at, h * 128 : (h + 1) * 128], qrot[h, at]], 1)
            s = lax.dot_general(left, right, NT, preferred_element_type=F32)
            if first or last:
                start, n = (0, OWN_FIRST * 64) if first else (OWN_FIRST * 64, OWN_LAST * 64)
                s = jnp.concatenate([s[:n] + hide[start : start + n, at], s[n:]], 0)
            return s

        def finish(h, at, s):
            w = jnp.exp2(s * SCALE2)
            sums = jnp.sum(w.reshape(CHUNK // 8, 8, at.stop - at.start), 0)
            vals = made[h // 2][1][(h % 2) * 128 : (h % 2 + 1) * 128]
            gains = jnp.dot(vals, w.astype(BF16), preferred_element_type=F32)
            if not first:
                sums = total[h, :, at] + sums
                gains = acc[h, :, at] + gains
            if not last:
                total[h, :, at] = sums
                acc[h, :, at] = gains
                return None
            row = jnp.sum(sums, 0, keepdims=True)
            done[at, h * 128 : (h + 1) * 128] = (gains / row).T.astype(BF16)
            return row

        def sweep(at, ahead):
            held = [scores(h, at) for h in range(ahead)]
            rows_total = []
            for h in range(HEADS):
                if h + ahead < HEADS:
                    held.append(scores(h + ahead, at))
                rows_total.append(finish(h, at, held.pop(0)))
            return rows_total

        if not last:
            sweep(slice(0, CHUNK), AHEAD)
            return
        for half in range(2):
            rows_total = sweep(slice(half * ROWS, (half + 1) * ROWS), 2 * AHEAD - 1)
            most = functools.reduce(jnp.maximum, rows_total)
            least = functools.reduce(jnp.minimum, rows_total)
            line = lax.broadcasted_iota(jnp.int32, (8, ROWS), 0)
            both = jnp.where(line < 4, most, least)
            if half:
                peak_ref[0] = both
                give.start()
            else:
                peak[...] = both
                give_away.start()
                tell.start()

    give = pltpu.make_async_copy(done.at[mine], fast.at[:, mine_cols], o_loc)
    give_away = remote(done.at[theirs], fast.at[:, mine_cols], o_send.at[0], o_recv.at[0], sibling)
    tell = remote(peak, peak_ref.at[1], o_send.at[1], o_recv.at[1], sibling)

    def keep(k):
        return pltpu.make_async_copy(lat.at[pl.ds(k * 8, 8)], all_hbm.at[pl.ds(k * 8, 8)], all_sem.at[k])

    keep(0).start()
    work(0, first=True)

    def arrive(slots):
        for i in slots:
            unit_in(i).wait_recv()

    def step_body(k, carry):
        @pl.when(k == 1)
        def _():
            arrive(list(range(8, 24)) + [Y2, Z2])
            share_chunk(1).start()
            share_chunk(2).start()
            for i in STAGES[2]:
                pass_unit(i).start()

        @pl.when(k == 3)
        def _():
            arrive(range(24, 40))
            share_chunk(3).start()
            share_chunk(4).start()
            for i in STAGES[3]:
                pass_unit(i).start()

        @pl.when(k == 5)
        def _():
            arrive(range(40, 56))
            share_chunk(5).start()
            share_chunk(6).start()

        @pl.when(k == 6)
        def _():
            arrive(range(58, 64))
            share_chunk(7).start()

        @pl.when(k % 2 == 0)
        def _():
            chunk_in(k - 1).wait_recv()
            chunk_in(k).wait_recv()
            keep(k - 1).start()
            keep(k).start()

        late = (k + 1) % 2
        work(k - late, side_now=core + late * (1 - 2 * core))
        return carry

    lax.fori_loop(1, 7, step_body, 0)

    chunk_in(7).wait_recv()
    keep(7).start()
    work(7, last=True)

    for c in swap:
        c.wait_send()

    def all_sent(i, carry):
        unit_in(i).wait_send()
        return carry

    lax.fori_loop(1, 64, all_sent, 0)
    for part in FIRST_SHARES:
        share(*part, core).wait_send()
    for k in range(1, 8):
        share_chunk(k).wait_send()
    for k in range(8):
        keep(k).wait()
    give.wait()
    give_away.wait_send()
    into = fast.at[:, their_cols]
    remote(into, into, o_send.at[0], o_recv.at[0], sibling).wait_recv()
    tell.wait()


def settle(
    peak, pos_ref, fast, all_hbm, qn_hbm, qr_hbm, wk_hbm, wv_hbm, out_hbm,
    lat, wk, wv, qn, qr, acc, total, top, result, sem, out_sem,
):
    whole = pltpu.make_async_copy(fast, out_hbm, out_sem)
    whole.start()
    line = lax.broadcasted_iota(jnp.int32, (2, 8, ROWS), 1)
    low = jnp.where(peak[...] <= 1.0, 1.0, 0.0)
    high = jnp.where(peak[...] >= LEAST, 1.0, 0.0)
    bad = jnp.min(jnp.where(line < 4, low, high)) < 0.5
    whole.wait()

    @pl.when(bad)
    def _():
        core = lax.axis_index("seq") % 2
        head = lax.axis_index("head")

        def fetch(src, dst):
            c = pltpu.make_async_copy(src, dst, sem)
            c.start()
            c.wait()

        fetch(all_hbm, lat)
        qmask = query_mask(pos_ref).astype(F32)
        qlane = lax.broadcasted_iota(jnp.int32, (ROWS, 128), 1)

        def one_pair(pair, carry):
            pair_cols = at_rows(pair * 256, 256, 256)
            fetch(wk_hbm.at[:, pair_cols], wk)
            fetch(wv_hbm.at[:, pair_cols], wv)
            fetch(qn_hbm.at[:, pair_cols], qn)
            fetch(qr_hbm.at[:, at_rows(pair * 128, 128, 128)], qr)
            for side in range(2):
                cols = slice(side * 128, (side + 1) * 128)
                both = qr[...].astype(F32)
                if side:
                    both = pltpu.roll(both, ROPE, 1)
                rot = jnp.where(qlane < ROPE, both, qmask).astype(BF16)
                right = jnp.concatenate([qn[:, cols], rot], 1)
                acc[...] = jnp.zeros_like(acc)
                total[...] = jnp.zeros_like(total)
                top[...] = jnp.full_like(top, MASKED)

                def one_block(i, c):
                    rows = lat[pl.ds(i * 4, 4)].reshape(ROWS, WIDE)
                    here = rows[:, :LATENT]
                    keys = jnp.dot(here, wk[:, cols], preferred_element_type=F32).astype(BF16)
                    vals = jnp.dot(here, wv[:, cols], preferred_element_type=F32).astype(BF16)
                    left = jnp.concatenate([keys, rows[:, LATENT:]], 1)
                    s = lax.dot_general(right, left, NT, preferred_element_type=F32)
                    q = lax.broadcasted_iota(jnp.int32, (ROWS, ROWS), 0)
                    k = lax.broadcasted_iota(jnp.int32, (ROWS, ROWS), 1)
                    slot = i * 4 + k // 64
                    h = jnp.full((ROWS, ROWS), 8, jnp.int32)
                    for own in list(range(OWN_FIRST)) + list(range(56, 56 + OWN_LAST)):
                        h = jnp.where(slot == own, head_of(own, head // 2, head % 2), h)
                    own_key = h * UNIT + k % UNIT
                    same = (h < 8) & (k // UNIT % 2 == core) & (own_key // 128 == q // 128)
                    s = jnp.where(same & (own_key > q), MASKED, s) * SCALE2
                    new = jnp.maximum(top[...], jnp.max(s, 1, keepdims=True))
                    w = jnp.where(s > MASKED * SCALE2 / 2, jnp.exp2(s - new[:, :1]), 0.0)
                    factor = jnp.exp2(top[...] - new)
                    total[...] = total[...] * factor + jnp.sum(w, 1, keepdims=True)
                    acc[...] = acc[...] * factor + jnp.dot(w.astype(BF16), vals, preferred_element_type=F32)
                    top[...] = new
                    return c

                lax.fori_loop(0, 16, one_block, 0)
                result[:, cols] = (acc[...] / total[...]).astype(BF16)
            fetch(result, out_hbm.at[:, pair_cols])
            return carry

        lax.fori_loop(0, 8, one_pair, 0)


def per_device(q_nope, q_rope, latent, k_rope, positions, w_uk, w_uv):
    hbm = pl.BlockSpec(memory_space=pltpu.HBM)
    vmem = pl.BlockSpec(memory_space=pltpu.VMEM)
    smem = pl.BlockSpec(memory_space=pltpu.SMEM)
    dma = pltpu.SemaphoreType.DMA
    fast, rows, peak = pl.pallas_call(
        gather_attend,
        out_shape=(
            pltpu.VMEM((ROWS, 2 * COLS), BF16),
            jax.ShapeDtypeStruct((64, 2, UNIT, WIDE), BF16),
            pltpu.VMEM((2, 8, ROWS), F32),
        ),
        in_specs=[smem, vmem, vmem] + [hbm] * 4,
        out_specs=(vmem, hbm, vmem),
        scratch_shapes=[
            pltpu.VMEM((64, 2, UNIT, WIDE), BF16),
            pltpu.VMEM((LATENT, COLS), BF16),
            pltpu.VMEM((LATENT, COLS), BF16),
            pltpu.VMEM((COLS, LATENT), BF16),
            pltpu.VMEM((CHUNK, COLS), BF16),
            pltpu.VMEM((CHUNK, COLS // 2), BF16),
            pltpu.VMEM((CHUNK, 128), BF16),
            pltpu.VMEM((HEADS, CHUNK, 128), BF16),
            pltpu.VMEM(((OWN_FIRST + OWN_LAST) * 64, CHUNK), F32),
            pltpu.VMEM((HEADS, 128, CHUNK), F32),
            pltpu.VMEM((HEADS, 8, CHUNK), F32),
            pltpu.VMEM((CHUNK, COLS), BF16),
            pltpu.VMEM((8, ROWS), F32),
            dma((4,)),
            dma((3,)), dma((3,)),
            dma((64,)), dma((64,)),
            dma((10,)), dma((10,)),
            dma,
            dma((2,)), dma((2,)),
            dma((8,)),
        ],
        compiler_params=pltpu.CompilerParams(
            collective_id=0, has_side_effects=True, vmem_limit_bytes=58 * 2**20
        ),
        cost_estimate=pl.CostEstimate(flops=26 * 10**9, bytes_accessed=12 * 2**20, transcendentals=17 * 10**6),
        name="gather_attend",
    )(positions, latent, k_rope, q_nope, q_rope, w_uk, w_uv)
    fast = pltpu.with_memory_space_constraint(fast, pltpu.VMEM)
    peak = pltpu.with_memory_space_constraint(peak, pltpu.VMEM)
    return pl.pallas_call(
        settle,
        out_shape=jax.ShapeDtypeStruct((ROWS, 2 * COLS), BF16),
        in_specs=[vmem, smem, vmem] + [hbm] * 5,
        out_specs=hbm,
        scratch_shapes=[
            pltpu.VMEM((64, 2, UNIT, WIDE), BF16),
            pltpu.VMEM((LATENT, 256), BF16),
            pltpu.VMEM((LATENT, 256), BF16),
            pltpu.VMEM((ROWS, 256), BF16),
            pltpu.VMEM((ROWS, 128), BF16),
            pltpu.VMEM((ROWS, 128), F32),
            pltpu.VMEM((ROWS, 128), F32),
            pltpu.VMEM((ROWS, 128), F32),
            pltpu.VMEM((ROWS, 256), BF16),
            dma,
            dma,
        ],
        compiler_params=pltpu.CompilerParams(vmem_limit_bytes=59 * 2**20),
        name="settle",
    )(peak, positions, fast, rows, q_nope, q_rope, w_uk, w_uv)


def solution(mesh):
    in_specs = (
        P("seq", "head"),
        P("seq", "head"),
        P(("seq", "head"), None),
        P(("seq", "head"), None),
        P("seq"),
        P(None, "head"),
        P(None, "head"),
    )
    return jax.shard_map(
        per_device, mesh=mesh, in_specs=in_specs, out_specs=P("seq", "head"), check_vma=False
    )
```

```python
import functools
import math

import jax
import jax.numpy as jnp
from jax import lax
from jax.experimental import pallas as pl
from jax.experimental.pallas import tpu as pltpu
from jax.sharding import PartitionSpec as P

MESH = pl.DeviceIdType.MESH
F32 = jnp.float32
BF16 = jnp.bfloat16
NT = (((1,), (1,)), ((), ()))
NOPE = 128
ROPE = 64
LATENT = 512
WIDE = 640
ROWS = 256
CHUNK = 512
PIECES = 8
UNIT = 32
HEADS = 8
AHEAD = 3
COLS = HEADS * NOPE
SCALE2 = (NOPE + ROPE) ** (-0.5) * math.log2(math.e)
MASKED = -1e30
SHIFT = 576.0
LEAST = 2.0**-90


def both_signs(pattern):
    found = [()]
    for p in pattern:
        found = [f + (v,) for f in found for v in ((1, 3) if p == 1 else (p,))]
    return found


SLOTS = (
    [(0, 0, 0), (0, 1, 0), (0, 3, 0), (1, 0, 0), (3, 0, 0), (0, 0, 1), (0, 0, 3), (2, 0, 0)]
    + both_signs((1, 1, 0)) + [(1, 0, 1), (3, 0, 3), (0, 1, 3), (0, 3, 1)]
    + [(1, 0, 3), (3, 0, 1), (0, 1, 1), (0, 3, 3)] + both_signs((2, 1, 0)) + both_signs((2, 0, 1))
    + both_signs((1, 2, 0)) + both_signs((0, 2, 1)) + both_signs((1, 0, 2)) + [(2, 2, 0), (2, 0, 2)]
    + both_signs((1, 1, 1))
    + both_signs((2, 1, 1)) + both_signs((1, 2, 1))
    + both_signs((1, 1, 2)) + both_signs((2, 2, 1)) + both_signs((1, 2, 2))
    + [(0, 2, 0), (0, 0, 2), (0, 1, 2), (0, 3, 2), (0, 2, 2), (2, 1, 2), (2, 3, 2), (2, 2, 2)]
)
Y2, Z2 = 56, 57
OWN_FIRST, OWN_LAST = 3, 5
STAGES = (
    list(range(1, 8)) + [Y2, Z2],
    list(range(8, 24)),
    list(range(24, 44)) + [58, 59, 60],
    list(range(44, 56)) + [61, 62, 63],
)


def plan_routes():
    place = {s: i for i, s in enumerate(SLOTS)}
    routes = {i: (SLOTS[i], 0) for i in STAGES[0]}
    have = {0}
    for stages, more in zip(STAGES[1:], (STAGES[0][:7], STAGES[1] + [Y2, Z2], list(range(24, 40)))):
        have |= set(more)
        load = {}
        options, taken = {}, {}
        for i in stages:
            options[i] = []
            for axis in range(3):
                for way in {0: (), 1: (1,), 3: (3,), 2: (1, 3, 2)}[SLOTS[i][axis]]:
                    step = tuple(way if a == axis else 0 for a in range(3))
                    parent = place[tuple((v - w) % 4 for v, w in zip(SLOTS[i], step))]
                    if parent in have:
                        links = [(axis, w) for w in ((1, 3) if way == 2 else (way,))]
                        options[i].append((step, parent, links))
            single = [o for o in options[i] if len(o[2]) == 1]
            options[i] = single or options[i]
        for i in stages * 6:
            for k in taken.get(i, ((), 0, ()))[2]:
                load[k] -= 1
            taken[i] = min(options[i], key=lambda o: (sum(load.get(k, 0) for k in o[2]) / len(o[2]), o[0], o[1]))
            for k in taken[i][2]:
                load[k] = load.get(k, 0) + 1
        for i in stages:
            routes[i] = taken[i][:2]
    return routes


ROUTES = plan_routes()
FIRST_SHARES = ((0, 4, 0), (4, 3, 8), (7, 1, 9))


def at_rows(start, size, step):
    return pl.ds(pl.multiple_of(start, step), size)


def key_lanes(shape, block):
    return jnp.where(lax.broadcasted_iota(jnp.int32, shape, 1) - ROPE == block, 1.0, 0.0)


def query_mask(pos_ref):
    parts = []
    for i in range(2):
        lane = lax.broadcasted_iota(jnp.int32, (128, 128), 1) - ROPE
        value = jnp.where(lane > pos_ref[i * 128] // 128, MASKED, -SHIFT)
        parts.append(jnp.where((lane >= 0) & (lane < 32), value, 0.0))
    return jnp.concatenate(parts, 0).astype(BF16)


def head_of(slot, y, zh):
    _, dy, dz = SLOTS[slot]
    return ((y + dy) % 4) * 2 + (zh + dz // 2) % 2


def gather_attend(
    pos_ref, lat_ref, rot_ref, qn_hbm, qr_hbm, wk_hbm, wv_hbm,
    fast, all_hbm, peak_ref,
    lat, wk, wv, wvt, qn, qr, qmask, qrot, hide, acc, total, done, peak,
    loc_sem, q_send, q_recv, u_send, u_recv, d_send, d_recv, o_loc, o_send, o_recv, all_sem,
):
    seq = lax.axis_index("seq")
    head = lax.axis_index("head")
    x, zl, core = seq // 4, (seq // 2) % 2, seq % 2
    y, zh = head // 2, head % 2
    z = zh * 2 + zl
    other = 1 - core

    def chip(back):
        px, py, pz = (x + 4 - back[0]) % 4, (y + 4 - back[1]) % 4, (z + 4 - back[2]) % 4
        return (px * 4 + (pz % 2) * 2 + core, py * 2 + pz // 2)

    sibling = (seq + 1 - 2 * core, head)
    near = STAGES[0]
    partners = [chip(SLOTS[i]) for i in near] + [sibling]

    barrier = pltpu.get_barrier_semaphore()
    for p in partners:
        pl.semaphore_signal(barrier, inc=1, device_id=p, device_id_type=MESH)

    theirs, mine = pl.ds(0, ROWS), pl.ds(ROWS, ROWS)
    mine_cols = at_rows(core * COLS, COLS, COLS)
    their_cols = at_rows(other * COLS, COLS, COLS)
    half_cols = COLS // 2
    local = [
        pltpu.make_async_copy(wv_hbm.at[:, mine_cols], wv, loc_sem.at[0]),
        pltpu.make_async_copy(wk_hbm.at[:, mine_cols], wk, loc_sem.at[1]),
        pltpu.make_async_copy(qn_hbm.at[:, mine_cols], qn.at[mine], loc_sem.at[2]),
        pltpu.make_async_copy(
            qr_hbm.at[:, at_rows(core * half_cols, half_cols, half_cols)], qr.at[mine], loc_sem.at[3]
        ),
    ]
    for c in local:
        c.start()

    block = jnp.where(head < 4, pos_ref[0] // 128, pos_ref[128] // 128)
    lane = lax.broadcasted_iota(jnp.int32, (UNIT, 128), 1)
    rot = jnp.concatenate([rot_ref[...].astype(F32), jnp.zeros((UNIT, ROPE), F32)], 1)
    lat[0, core, :, :LATENT] = lat_ref[...]
    lat[0, core, :, LATENT:] = jnp.where(lane < ROPE, rot, key_lanes((UNIT, 128), block)).astype(BF16)
    qmask[mine] = query_mask(pos_ref)

    pl.semaphore_wait(barrier, len(partners))

    def remote(src, dst, send, recv, to):
        return pltpu.make_async_remote_copy(
            src_ref=src, dst_ref=dst, send_sem=send, recv_sem=recv, device_id=to, device_id_type=MESH
        )

    def pass_unit(i):
        step, parent = ROUTES[i]
        return remote(lat.at[parent, core], lat.at[i, core], u_send.at[i], u_recv.at[i], chip(step))

    def unit_in(i):
        ref = lat.at[i, core]
        return remote(ref, ref, u_send.at[i], u_recv.at[i], sibling)

    def share(i, size, sem, side):
        ref = lat.at[pl.ds(i, size), side]
        return remote(ref, ref, d_send.at[sem], d_recv.at[sem], sibling)

    def share_chunk(k):
        return share(k * 8, 8, k, core)

    def chunk_in(k):
        return share(k * 8, 8, k, other)

    for i in STAGES[0]:
        pass_unit(i).start()
    swap = [
        remote(qn_hbm.at[:, their_cols], qn.at[theirs], q_send.at[0], q_recv.at[0], sibling),
        remote(
            qr_hbm.at[:, at_rows(other * half_cols, half_cols, half_cols)], qr.at[theirs],
            q_send.at[1], q_recv.at[1], sibling,
        ),
        remote(qmask.at[mine], qmask.at[theirs], q_send.at[2], q_recv.at[2], sibling),
    ]
    for c in swap:
        c.start()
    swap_in = [
        remote(qn.at[theirs], qn.at[theirs], q_send.at[0], q_recv.at[0], sibling),
        remote(qr.at[theirs], qr.at[theirs], q_send.at[1], q_recv.at[1], sibling),
        remote(qmask.at[theirs], qmask.at[theirs], q_send.at[2], q_recv.at[2], sibling),
    ]

    qlane = lax.broadcasted_iota(jnp.int32, (ROWS, 128), 1)

    def prepare(rows):
        mask_rows = qmask[rows].astype(F32)
        for pair in range(HEADS // 2):
            both = qr[rows, pair * 128 : (pair + 1) * 128].astype(F32)
            qrot[2 * pair, rows] = jnp.where(qlane < ROPE, both, mask_rows).astype(BF16)
            qrot[2 * pair + 1, rows] = jnp.where(qlane < ROPE, pltpu.roll(both, ROPE, 1), mask_rows).astype(BF16)

    local[2].wait()
    local[3].wait()
    prepare(mine)
    key = lax.broadcasted_iota(jnp.int32, (UNIT, CHUNK), 0)
    query = lax.broadcasted_iota(jnp.int32, (UNIT, CHUNK), 1)
    query = query + jnp.where(query < ROWS, other * ROWS, (core - 1) * ROWS)
    for n, slot in enumerate(list(range(OWN_FIRST)) + list(range(56, 56 + OWN_LAST))):
        h = head_of(slot, y, zh)
        for side in range(2):
            hidden = (query // 128 == side * 2 + h // 4) & (key + side * ROWS + h * UNIT > query)
            hide[(n * 2 + side) * UNIT : (n * 2 + side + 1) * UNIT, :] = jnp.where(hidden, MASKED, 0.0)
    local[0].wait()
    for i in range(HEADS):
        wvt[i * 128 : (i + 1) * 128, :] = wv[:, i * 128 : (i + 1) * 128].T
    local[1].wait()
    for c in swap_in:
        c.wait_recv()
    prepare(theirs)

    for i in STAGES[0][:7]:
        unit_in(i).wait_recv()
        for j in STAGES[1]:
            if ROUTES[j][1] == i:
                pass_unit(j).start()
        for part in FIRST_SHARES:
            if part[0] + part[1] == i + 1:
                share(*part, core).start()
    for part in FIRST_SHARES:
        share(*part, other).wait_recv()

    def work(k, side_now=None, first=False, last=False):
        made = {}

        def lanes(a, b):
            if side_now is None:
                return lat[pl.ds(k * 8, 8), :, :, a:b].reshape(CHUNK, b - a)
            return lat[pl.ds(k * 8, 16), side_now, :, a:b].reshape(CHUNK, b - a)

        def scores(h, at):
            pair, side = h // 2, h % 2
            if pair not in made:
                cols = slice(pair * 256, (pair + 1) * 256)
                here = lanes(0, LATENT)
                keys = jnp.dot(here, wk[:, cols], preferred_element_type=F32).astype(BF16)
                vals = lax.dot_general(wvt[cols, :], here, NT, preferred_element_type=F32).astype(BF16)
                made[pair] = (keys, vals)
            keys = made[pair][0][:, side * 128 : (side + 1) * 128]
            left = jnp.concatenate([keys, lanes(LATENT, WIDE)], 1)
            right = jnp.concatenate([qn[at, h * 128 : (h + 1) * 128], qrot[h, at]], 1)
            s = lax.dot_general(left, right, NT, preferred_element_type=F32)
            if first or last:
                start, n = (0, OWN_FIRST * 64) if first else (OWN_FIRST * 64, OWN_LAST * 64)
                s = jnp.concatenate([s[:n] + hide[start : start + n, at], s[n:]], 0)
            return s

        def finish(h, at, s):
            w = jnp.exp2(s * SCALE2)
            sums = jnp.sum(w.reshape(CHUNK // 8, 8, at.stop - at.start), 0)
            vals = made[h // 2][1][(h % 2) * 128 : (h % 2 + 1) * 128]
            gains = jnp.dot(vals, w.astype(BF16), preferred_element_type=F32)
            if not first:
                sums = total[h, :, at] + sums
                gains = acc[h, :, at] + gains
            if not last:
                total[h, :, at] = sums
                acc[h, :, at] = gains
                return None
            row = jnp.sum(sums, 0, keepdims=True)
            done[at, h * 128 : (h + 1) * 128] = (gains / row).T.astype(BF16)
            return row

        def sweep(at, ahead):
            held = [scores(h, at) for h in range(ahead)]
            rows_total = []
            for h in range(HEADS):
                if h + ahead < HEADS:
                    held.append(scores(h + ahead, at))
                rows_total.append(finish(h, at, held.pop(0)))
            return rows_total

        if not last:
            sweep(slice(0, CHUNK), AHEAD)
            return
        for half in range(2):
            rows_total = sweep(slice(half * ROWS, (half + 1) * ROWS), 2 * AHEAD - 1)
            most = functools.reduce(jnp.maximum, rows_total)
            least = functools.reduce(jnp.minimum, rows_total)
            line = lax.broadcasted_iota(jnp.int32, (8, ROWS), 0)
            both = jnp.where(line < 4, most, least)
            if half:
                peak_ref[0] = both
                for c in give:
                    c.start()
            else:
                peak[...] = both
                give_away.start()
                tell.start()

    give = []
    for i in range(PIECES):
        size = ROWS // PIECES
        src = done.at[pl.ds(ROWS + i * size, size)]
        give.append(pltpu.make_async_copy(src, fast.at[pl.ds(i * size, size), mine_cols], o_loc.at[i]))
    give_away = remote(done.at[theirs], fast.at[:, mine_cols], o_send.at[0], o_recv.at[0], sibling)
    tell = remote(peak, peak_ref.at[1], o_send.at[1], o_recv.at[1], sibling)

    def keep(k):
        return pltpu.make_async_copy(lat.at[pl.ds(k * 8, 8)], all_hbm.at[pl.ds(k * 8, 8)], all_sem.at[k])

    keep(0).start()
    work(0, first=True)

    def arrive(slots):
        for i in slots:
            unit_in(i).wait_recv()

    def step_body(k, carry):
        @pl.when(k == 1)
        def _():
            arrive(list(range(8, 24)) + [Y2, Z2])
            share_chunk(1).start()
            share_chunk(2).start()
            for i in STAGES[2]:
                pass_unit(i).start()

        @pl.when(k == 3)
        def _():
            arrive(range(24, 40))
            share_chunk(3).start()
            share_chunk(4).start()
            for i in STAGES[3]:
                pass_unit(i).start()

        @pl.when(k == 5)
        def _():
            arrive(range(40, 56))
            share_chunk(5).start()
            share_chunk(6).start()

        @pl.when(k == 6)
        def _():
            arrive(range(58, 64))
            share_chunk(7).start()

        @pl.when(k % 2 == 0)
        def _():
            chunk_in(k - 1).wait_recv()
            chunk_in(k).wait_recv()
            keep(k - 1).start()
            keep(k).start()

        late = (k + 1) % 2
        work(k - late, side_now=core + late * (1 - 2 * core))
        return carry

    lax.fori_loop(1, 7, step_body, 0)

    chunk_in(7).wait_recv()
    keep(7).start()
    work(7, last=True)

    for c in swap:
        c.wait_send()

    def all_sent(i, carry):
        unit_in(i).wait_send()
        return carry

    lax.fori_loop(1, 64, all_sent, 0)
    for part in FIRST_SHARES:
        share(*part, core).wait_send()
    for k in range(1, 8):
        share_chunk(k).wait_send()
    for k in range(8):
        keep(k).wait()
    for c in give:
        c.wait()
    give_away.wait_send()
    into = fast.at[:, their_cols]
    remote(into, into, o_send.at[0], o_recv.at[0], sibling).wait_recv()
    tell.wait()


def settle(
    peak, pos_ref, fast, all_hbm, qn_hbm, qr_hbm, wk_hbm, wv_hbm, out_hbm,
    lat, wk, wv, qn, qr, acc, total, top, result, sem, out_sem,
):
    pieces = []
    for i in range(PIECES):
        rows = pl.ds(i * (ROWS // PIECES), ROWS // PIECES)
        pieces.append(pltpu.make_async_copy(fast.at[rows], out_hbm.at[rows], out_sem.at[i]))
    for c in pieces:
        c.start()
    line = lax.broadcasted_iota(jnp.int32, (2, 8, ROWS), 1)
    low = jnp.where(peak[...] <= 1.0, 1.0, 0.0)
    high = jnp.where(peak[...] >= LEAST, 1.0, 0.0)
    bad = jnp.min(jnp.where(line < 4, low, high)) < 0.5
    for c in pieces:
        c.wait()

    @pl.when(bad)
    def _():
        core = lax.axis_index("seq") % 2
        head = lax.axis_index("head")

        def fetch(src, dst):
            c = pltpu.make_async_copy(src, dst, sem)
            c.start()
            c.wait()

        fetch(all_hbm, lat)
        qmask = query_mask(pos_ref).astype(F32)
        qlane = lax.broadcasted_iota(jnp.int32, (ROWS, 128), 1)

        def one_pair(pair, carry):
            pair_cols = at_rows(pair * 256, 256, 256)
            fetch(wk_hbm.at[:, pair_cols], wk)
            fetch(wv_hbm.at[:, pair_cols], wv)
            fetch(qn_hbm.at[:, pair_cols], qn)
            fetch(qr_hbm.at[:, at_rows(pair * 128, 128, 128)], qr)
            for side in range(2):
                cols = slice(side * 128, (side + 1) * 128)
                both = qr[...].astype(F32)
                if side:
                    both = pltpu.roll(both, ROPE, 1)
                rot = jnp.where(qlane < ROPE, both, qmask).astype(BF16)
                right = jnp.concatenate([qn[:, cols], rot], 1)
                acc[...] = jnp.zeros_like(acc)
                total[...] = jnp.zeros_like(total)
                top[...] = jnp.full_like(top, MASKED)

                def one_block(i, c):
                    rows = lat[pl.ds(i * 4, 4)].reshape(ROWS, WIDE)
                    here = rows[:, :LATENT]
                    keys = jnp.dot(here, wk[:, cols], preferred_element_type=F32).astype(BF16)
                    vals = jnp.dot(here, wv[:, cols], preferred_element_type=F32).astype(BF16)
                    left = jnp.concatenate([keys, rows[:, LATENT:]], 1)
                    s = lax.dot_general(right, left, NT, preferred_element_type=F32)
                    q = lax.broadcasted_iota(jnp.int32, (ROWS, ROWS), 0)
                    k = lax.broadcasted_iota(jnp.int32, (ROWS, ROWS), 1)
                    slot = i * 4 + k // 64
                    h = jnp.full((ROWS, ROWS), 8, jnp.int32)
                    for own in list(range(OWN_FIRST)) + list(range(56, 56 + OWN_LAST)):
                        h = jnp.where(slot == own, head_of(own, head // 2, head % 2), h)
                    own_key = h * UNIT + k % UNIT
                    same = (h < 8) & (k // UNIT % 2 == core) & (own_key // 128 == q // 128)
                    s = jnp.where(same & (own_key > q), MASKED, s) * SCALE2
                    new = jnp.maximum(top[...], jnp.max(s, 1, keepdims=True))
                    w = jnp.where(s > MASKED * SCALE2 / 2, jnp.exp2(s - new[:, :1]), 0.0)
                    factor = jnp.exp2(top[...] - new)
                    total[...] = total[...] * factor + jnp.sum(w, 1, keepdims=True)
                    acc[...] = acc[...] * factor + jnp.dot(w.astype(BF16), vals, preferred_element_type=F32)
                    top[...] = new
                    return c

                lax.fori_loop(0, 16, one_block, 0)
                result[:, cols] = (acc[...] / total[...]).astype(BF16)
            fetch(result, out_hbm.at[:, pair_cols])
            return carry

        lax.fori_loop(0, 8, one_pair, 0)


def per_device(q_nope, q_rope, latent, k_rope, positions, w_uk, w_uv):
    hbm = pl.BlockSpec(memory_space=pltpu.HBM)
    vmem = pl.BlockSpec(memory_space=pltpu.VMEM)
    smem = pl.BlockSpec(memory_space=pltpu.SMEM)
    dma = pltpu.SemaphoreType.DMA
    fast, rows, peak = pl.pallas_call(
        gather_attend,
        out_shape=(
            pltpu.VMEM((ROWS, 2 * COLS), BF16),
            jax.ShapeDtypeStruct((64, 2, UNIT, WIDE), BF16),
            pltpu.VMEM((2, 8, ROWS), F32),
        ),
        in_specs=[smem, vmem, vmem] + [hbm] * 4,
        out_specs=(vmem, hbm, vmem),
        scratch_shapes=[
            pltpu.VMEM((64, 2, UNIT, WIDE), BF16),
            pltpu.VMEM((LATENT, COLS), BF16),
            pltpu.VMEM((LATENT, COLS), BF16),
            pltpu.VMEM((COLS, LATENT), BF16),
            pltpu.VMEM((CHUNK, COLS), BF16),
            pltpu.VMEM((CHUNK, COLS // 2), BF16),
            pltpu.VMEM((CHUNK, 128), BF16),
            pltpu.VMEM((HEADS, CHUNK, 128), BF16),
            pltpu.VMEM(((OWN_FIRST + OWN_LAST) * 64, CHUNK), F32),
            pltpu.VMEM((HEADS, 128, CHUNK), F32),
            pltpu.VMEM((HEADS, 8, CHUNK), F32),
            pltpu.VMEM((CHUNK, COLS), BF16),
            pltpu.VMEM((8, ROWS), F32),
            dma((4,)),
            dma((3,)), dma((3,)),
            dma((64,)), dma((64,)),
            dma((10,)), dma((10,)),
            dma((PIECES,)),
            dma((2,)), dma((2,)),
            dma((8,)),
        ],
        compiler_params=pltpu.CompilerParams(
            collective_id=0, has_side_effects=True, vmem_limit_bytes=58 * 2**20
        ),
        cost_estimate=pl.CostEstimate(flops=26 * 10**9, bytes_accessed=12 * 2**20, transcendentals=17 * 10**6),
        name="gather_attend",
    )(positions, latent, k_rope, q_nope, q_rope, w_uk, w_uv)
    fast = pltpu.with_memory_space_constraint(fast, pltpu.VMEM)
    peak = pltpu.with_memory_space_constraint(peak, pltpu.VMEM)
    return pl.pallas_call(
        settle,
        out_shape=jax.ShapeDtypeStruct((ROWS, 2 * COLS), BF16),
        in_specs=[vmem, smem, vmem] + [hbm] * 5,
        out_specs=hbm,
        scratch_shapes=[
            pltpu.VMEM((64, 2, UNIT, WIDE), BF16),
            pltpu.VMEM((LATENT, 256), BF16),
            pltpu.VMEM((LATENT, 256), BF16),
            pltpu.VMEM((ROWS, 256), BF16),
            pltpu.VMEM((ROWS, 128), BF16),
            pltpu.VMEM((ROWS, 128), F32),
            pltpu.VMEM((ROWS, 128), F32),
            pltpu.VMEM((ROWS, 128), F32),
            pltpu.VMEM((ROWS, 256), BF16),
            dma,
            dma((PIECES,)),
        ],
        compiler_params=pltpu.CompilerParams(vmem_limit_bytes=59 * 2**20),
        name="settle",
    )(peak, positions, fast, rows, q_nope, q_rope, w_uk, w_uv)


def solution(mesh):
    in_specs = (
        P("seq", "head"),
        P("seq", "head"),
        P(("seq", "head"), None),
        P(("seq", "head"), None),
        P("seq"),
        P(None, "head"),
        P(None, "head"),
    )
    return jax.shard_map(
        per_device, mesh=mesh, in_specs=in_specs, out_specs=P("seq", "head"), check_vma=False
    )
```
